512 devices in a mesh: gx: 32 (over z_lo, y), gy: 16 (over x, z_hi, core).
Axes of the slice: x: 4, y: 4, z: 16 (z_hi: 2, z_lo: 8; z = z_hi * 8 + z_lo), core: 2. Of those that a mesh axis runs over, the one named last changes fastest.
Arguments:
- velocity: float32 [64, 256, 2048], P('gy', 'gx'), may hold values from -6 to 6
Outputs:
- coefficients: float32 [64, 256, 2048], P(None, 'gx', 'gy')
The draws below stay inside these ranges and needn't reach their ends.
All inputs are finite; a program needn't handle non-finite values.
Results may differ from the reference program's by a relative error of at most 0.00007.
Values sent between devices are 32-bit elements; how exact they have to be, the bound alone decides.
A program may use at most 64 MiB of HBM per device.

```python
import jax
import jax.numpy as jnp
from jax import lax

NZ = 64
NX = 256
NY = 2048


def level_of(rng, extent, shards, smallest, high):
    gain = 1.0
    for dim, blocks in shards:
        steps = jax.random.uniform(jax.random.fold_in(jax.random.fold_in(rng, 6), dim), (blocks,), jnp.float32, smallest / len(shards), high / len(shards))
        gain = gain * jnp.repeat(jnp.exp(steps), extent[dim] // blocks).reshape((-1,) + (1,) * (len(extent) - 1 - dim))
    return gain


def bell_draw(key, dims, width, bound, cuts=(), dtype=jnp.bfloat16):
    level = level_of(key, dims, cuts, -0.22, 0.18) if cuts else 1.0
    entries = jax.random.normal(key, dims, jnp.float32) * width * level
    return jnp.minimum(jnp.maximum(entries, -bound), bound).astype(dtype)


def setup_inputs(seed: int = 0) -> dict:
    splits = jax.random.split(jax.random.key(seed), 2)
    velocity = bell_draw(splits[0], (NZ, NX, NY), 1.0, 6.0, ((0, 16), (1, 32)), jnp.float32)
    return dict(velocity=velocity)


PREDICT_FIRST = -1.586134342
UPDATE_FIRST = -0.05298011854
PREDICT_SECOND = 0.8829110762
UPDATE_SECOND = 0.4435068522
SCALE_LOW = 1.149604398
SCALE_HIGH = 1.0 / 1.149604398


def split_pairs(values, which_dim):
    length = values.shape[which_dim]
    even_part = lax.slice_in_dim(values, 0, length, 2, which_dim)
    odd_part = lax.slice_in_dim(values, 1, length, 2, which_dim)
    return even_part, odd_part


def lifting_steps(even_part, odd_part, which_dim):
    odd_part = odd_part + PREDICT_FIRST * (even_part + jnp.roll(even_part, -1, which_dim))
    even_part = even_part + UPDATE_FIRST * (odd_part + jnp.roll(odd_part, 1, which_dim))
    odd_part = odd_part + PREDICT_SECOND * (even_part + jnp.roll(even_part, -1, which_dim))
    even_part = even_part + UPDATE_SECOND * (odd_part + jnp.roll(odd_part, 1, which_dim))
    return even_part * SCALE_LOW, odd_part * SCALE_HIGH


def join_pairs(even_part, odd_part, which_dim):
    stacked = jnp.stack((even_part, odd_part), axis=which_dim + 1)
    new_shape = list(even_part.shape)
    new_shape[which_dim] = new_shape[which_dim] * 2
    return stacked.reshape(new_shape)


def lift_periodic(values, which_dim):
    even_part, odd_part = split_pairs(values, which_dim)
    even_part, odd_part = lifting_steps(even_part, odd_part, which_dim)
    return join_pairs(even_part, odd_part, which_dim)


def three_passes(values):
    values = lift_periodic(values, 2)
    values = lift_periodic(values, 1)
    return lift_periodic(values, 0)


def reference(velocity):
    level_one = three_passes(velocity)
    coarse = level_one[::2, ::2, ::2]
    coarse = three_passes(coarse)
    return level_one.at[::2, ::2, ::2].set(coarse)
```

```python
import functools

import jax
import jax.numpy as jnp
import numpy as np
from jax import lax
from jax.experimental import pallas as pl
from jax.experimental.pallas import tpu as pltpu
from jax.sharding import PartitionSpec as P

PREDICT_FIRST = -1.586134342
UPDATE_FIRST = -0.05298011854
PREDICT_SECOND = 0.8829110762
UPDATE_SECOND = 0.4435068522
SCALE_LOW = 1.149604398
SCALE_HIGH = 1.0 / 1.149604398

MESH = pl.DeviceIdType.MESH
ROWS = 8
TILE = 128
F32 = jnp.float32


def lift_matrix(extent):
    table = np.eye(extent)
    s, r = table[0::2], table[1::2]
    r = r + PREDICT_FIRST * (s + np.roll(s, -1, 0))
    s = s + UPDATE_FIRST * (r + np.roll(r, 1, 0))
    r = r + PREDICT_SECOND * (s + np.roll(s, -1, 0))
    s = s + UPDATE_SECOND * (r + np.roll(r, 1, 0))
    out = np.empty((extent, extent))
    out[0::2], out[1::2] = s * SCALE_LOW, r * SCALE_HIGH
    return out


def row_operators():
    extent, mine = 128, 64
    first = lift_matrix(extent)
    second = lift_matrix(extent // 2) @ first[0::2]
    wide = np.zeros((extent, extent))
    wide[0::2] = second

    def block(table, step):
        start = mine + ROWS * step
        return table[start : start + ROWS, mine : mine + ROWS]

    return {step: block(first, step) for step in (-1, 0, 1)}, {step: block(wide, step) for step in (-2, -1, 0, 1, 2)}


def coefficient_columns():
    first, second = row_operators()
    rows = np.arange(ROWS)
    columns, names = [], {}

    def add(name, column):
        if np.any(column != 0):
            names[name] = len(columns)
            columns.append(column)

    halo = first[1] + first[-1]
    assert not np.any((first[1] != 0) & (first[-1] != 0).any(axis=1, keepdims=True))
    for k in range(ROWS):
        source = (rows - k) % ROWS
        add(("own", k), first[0][rows, source])
        add(("halo", k), halo[rows, source])
        even = rows - rows % 2
        source = (even - k) % ROWS
        for step in (-1, 0, 1, 2):
            add((step, k), second[step][even, source])
    tail = np.zeros(ROWS)
    tail[4:] = second[-2][[4, 4, 6, 6], 0]
    add(("tail", 0), tail)
    table = np.zeros((ROWS, TILE), np.float32)
    table[:, : len(columns)] = np.stack(columns, 1)
    return table, names


COLUMNS, NAMES = coefficient_columns()


def lane_lift(value, stride):
    length = value.shape[-1]
    lane = lax.broadcasted_iota(jnp.int32, value.shape, value.ndim - 1)
    odd = (lane // stride) % 2 == 1

    def step(v, weight, mask_odd):
        near = pltpu.roll(v, stride, v.ndim - 1) + pltpu.roll(v, length - stride, v.ndim - 1)
        change = weight * near
        return v + (jnp.where(odd, change, 0.0) if mask_odd else jnp.where(odd, 0.0, change))

    value = step(value, PREDICT_FIRST, True)
    value = step(value, UPDATE_FIRST, False)
    value = step(value, PREDICT_SECOND, True)
    value = step(value, UPDATE_SECOND, False)
    return value * jnp.where(odd, SCALE_HIGH, SCALE_LOW)


def leading_lift(s, r):
    def after(a):
        return jnp.concatenate([a[1:], a[:1]], axis=0)

    def before(a):
        return jnp.concatenate([a[-1:], a[:-1]], axis=0)

    r = r + PREDICT_FIRST * (s + after(s))
    s = s + UPDATE_FIRST * (r + before(r))
    r = r + PREDICT_SECOND * (s + after(s))
    s = s + UPDATE_SECOND * (r + before(r))
    return s * SCALE_LOW, r * SCALE_HIGH


def kernel(nx, ny, v_hbm, table_hbm, out_ref, v_ref, table_ref, y_one, y_two, own, own_two, far_two, near_two, go_right,
           go_left, go_right_two, go_left_two, from_left, from_right, from_left_two, from_right_two, tail_two, send, got,
           in_sem, halo_send, halo_recv, send_sem, recv_sem):
    gx, gy = lax.axis_index("gx"), lax.axis_index("gy")
    half = (gy // 2) % 2
    blocks = ny // 4
    width = 2 * blocks * TILE

    load = pltpu.make_async_copy(v_hbm, v_ref, in_sem.at[0])
    load.start()
    load_table = pltpu.make_async_copy(table_hbm, table_ref, in_sem.at[1])
    load_table.start()

    def beside(step):
        return (lax.rem(gx + step + nx, nx), gy)

    def peer(side, j):
        block = lax.rem(gy // 4 + j // 2, blocks)
        core = lax.rem(gy + j, 2)
        return block, core, block * 4 + side * 2 + core

    barrier = pltpu.get_barrier_semaphore()
    far, near = 1 - half, half
    for step in (1, -1, 2, -2):
        pl.semaphore_signal(barrier, inc=1, device_id=beside(step), device_id_type=MESH)
    for side, first in ((far, 0), (near, 1)):
        for j in range(first, 2 * blocks):
            pl.semaphore_signal(barrier, inc=1, device_id=(gx, peer(side, j)[2]), device_id_type=MESH)

    load.wait()
    load_table.wait()

    @pl.loop(0, 4)
    def _(z):
        y_one[z] = lane_lift(v_ref[z], 1)

    @pl.loop(0, 2)
    def _(pair):
        a, b = y_one[2 * pair], y_one[2 * pair + 1]
        lane = lax.broadcasted_iota(jnp.int32, a.shape, 1)
        y_two[pair] = lane_lift(jnp.where(lane % 2 == 1, pltpu.roll(b, 1, 1), a), 2)

    row = lax.broadcasted_iota(jnp.int32, (ROWS, TILE), 0)
    low_row = row < 4
    even_row = row % 2 == 0

    def column(name):
        at = NAMES[name]
        return jnp.broadcast_to(table_ref[:, at : at + 1], (ROWS, TILE))

    def weigh(total, name, value):
        if name not in NAMES:
            return total
        term = column(name) * value
        return term if total is None else total + term

    def down(value, k):
        return value if k % ROWS == 0 else pltpu.roll(value, k % ROWS, 0)

    def x_pass(side):
        @pl.loop(0, 2 * blocks)
        def _(p):
            tile = (p // 2) * 4 + side * 2 + p % 2
            lanes = pl.ds(pl.multiple_of(tile * TILE, TILE), TILE)
            here = pl.ds(pl.multiple_of(p * TILE, TILE), TILE)
            halos = []
            for z in range(4):
                value = y_one[z, :, lanes]
                mine, halo = None, None
                for k in range(ROWS):
                    moved = down(value, k)
                    mine = weigh(mine, ("own", k), moved)
                    halo = weigh(halo, ("halo", k), moved)
                own[side, z, :, here] = mine
                halos.append(halo)
            for pair in range(2):
                a, b = halos[2 * pair], halos[2 * pair + 1]
                go_right[side, pair, :, here] = jnp.where(low_row, a, down(b, 4))
                go_left[side, pair, :, here] = jnp.where(low_row, down(a, 4), b)
            a, b = y_two[0, :, lanes], y_two[1, :, lanes]
            sums = {step: None for step in (-1, 0, 1, 2)}
            for k in range(ROWS):
                moved = jnp.where(even_row, down(a, k), down(b, k + 1))
                if k == 0:
                    near_two[side, :, here] = moved
                for step in sums:
                    sums[step] = weigh(sums[step], (step, k), moved)
            own_two[side, :, here] = sums[0]
            go_right[side, 2, :, here] = sums[1]
            go_left[side, 2, :, here] = sums[-1]
            far_two[side, :, here] = sums[2]

    wide_row = lax.broadcasted_iota(jnp.int32, (ROWS, 2 * TILE), 0)

    def pack_two(side):
        for source, target in ((far_two, go_right_two), (near_two, go_left_two)):
            packed = source[side, :, 0 : 2 * TILE]
            for block in range(1, blocks):
                value = down(source[side, :, block * 2 * TILE : (block + 1) * 2 * TILE], 2 * block)
                packed = jnp.where(wide_row // 2 == block, value, packed)
            target[side] = packed

    def halo_copies(side):
        copies = []
        for n, (source, target, step) in enumerate((
            (go_right, from_left, 1),
            (go_left, from_right, -1),
            (go_right_two, from_left_two, 2),
            (go_left_two, from_right_two, -2),
        )):
            copies.append(pltpu.make_async_remote_copy(
                src_ref=source.at[side],
                dst_ref=target.at[side],
                send_sem=halo_send.at[side, n],
                recv_sem=halo_recv.at[side, n],
                device_id=beside(step),
                device_id_type=MESH,
            ))
        return copies

    def unpack_two(side):
        tail = NAMES[("tail", 0)]
        weights = jnp.broadcast_to(table_ref[:, tail : tail + 1], (ROWS, 2 * TILE))
        for block in range(blocks):
            head = jnp.where(wide_row < 2, down(from_left_two[side], ROWS - 2 * block), 0.0)
            late = from_right_two[side]
            late = jnp.where(wide_row < 6, down(late, 4 - 2 * block), down(late, 6 - 2 * block))
            tail_two[side, :, block * 2 * TILE : (block + 1) * 2 * TILE] = head + weights * late

    def combine(side, block, core, target, slot):
        here = pl.ds(pl.multiple_of((block * 2 + core) * TILE, TILE), TILE)
        for pair in range(2):
            a, b = from_left[side, pair, :, here], from_right[side, pair, :, here]
            target[slot, 2 * pair] = own[side, 2 * pair, :, here] + jnp.where(low_row, a, down(b, 4))
            target[slot, 2 * pair + 1] = own[side, 2 * pair + 1, :, here] + jnp.where(low_row, down(a, 4), b)
        target[slot, 4] = (own_two[side, :, here] + tail_two[side, :, here]) + (
            from_left[side, 2, :, here] + from_right[side, 2, :, here])

    def tile_copy(tile):
        return pltpu.make_async_remote_copy(
            src_ref=send.at[tile],
            dst_ref=got.at[gy],
            send_sem=send_sem.at[tile],
            recv_sem=recv_sem.at[gy],
            device_id=(gx, tile),
            device_id_type=MESH,
        )

    def arrival(tile):
        return pltpu.make_async_remote_copy(
            src_ref=send.at[tile],
            dst_ref=got.at[tile],
            send_sem=send_sem.at[tile],
            recv_sem=recv_sem.at[tile],
            device_id=(gx, tile),
            device_id_type=MESH,
        )

    x_pass(far)
    pack_two(far)
    pl.semaphore_wait(barrier, 4 + 4 * blocks - 1)
    far_copies = halo_copies(far)
    for copy in far_copies:
        copy.start()
    x_pass(near)
    pack_two(near)
    near_copies = halo_copies(near)
    for copy in near_copies:
        copy.start()

    for copy in far_copies:
        copy.wait_recv()
    unpack_two(far)

    @pl.loop(0, 2 * blocks)
    def _(j):
        block, core, tile = peer(far, j)
        combine(far, block, core, send, tile)
        tile_copy(tile).start()

    for copy in near_copies:
        copy.wait_recv()
    unpack_two(near)

    @pl.loop(1, 2 * blocks)
    def _(j):
        block, core, tile = peer(near, j)
        combine(near, block, core, send, tile)
        tile_copy(tile).start()

    combine(near, gy // 4, lax.rem(gy, 2), got, gy)

    for copy in far_copies + near_copies:
        copy.wait_send()

    @pl.loop(1, 2 * blocks)
    def _(j):
        arrival(peer(near, j)[2]).wait()

    @pl.loop(0, 2 * blocks)
    def _(j):
        arrival(peer(far, j)[2]).wait()

    pairs = 2 * ny
    shape = (pairs, ROWS, TILE)
    s, r = leading_lift(got[:, 0:4:2].reshape(shape), got[:, 1:4:2].reshape(shape))
    slot = got[:, 4]
    under = pltpu.roll(slot, ROWS - 1, 1)

    def left(value):
        return pltpu.roll(value, TILE - 1, 2)

    even = jnp.stack([slot, under], axis=1).reshape(shape)
    odd = jnp.stack([left(slot), left(under)], axis=1).reshape(shape)
    coarse = leading_lift(even, odd)[0].reshape(ny, 2, ROWS, TILE)
    low, high = leading_lift(coarse[:, 0], coarse[:, 1])
    coarse = jnp.stack([low, high], axis=1).reshape(shape)
    corner = (lax.broadcasted_iota(jnp.int32, shape, 1) % 2 == 0) & (lax.broadcasted_iota(jnp.int32, shape, 2) % 2 == 0)
    out_ref[:, 0] = jnp.where(corner, coarse, s)
    out_ref[:, 1] = r


def solution(mesh):
    nx, ny = mesh.shape["gx"], mesh.shape["gy"]
    length = ny * TILE
    half = length // 2

    def body(velocity):
        out = pl.pallas_call(
            functools.partial(kernel, nx, ny),
            out_shape=jax.ShapeDtypeStruct((2 * ny, 2, ROWS, TILE), F32),
            in_specs=[pl.BlockSpec(memory_space=pl.ANY)] * 2,
            out_specs=pl.BlockSpec(memory_space=pltpu.VMEM),
            scratch_shapes=[
                pltpu.VMEM((4, ROWS, length), F32),
                pltpu.VMEM((ROWS, TILE), F32),
                pltpu.VMEM((4, ROWS, length), F32),
                pltpu.VMEM((2, ROWS, length), F32),
                pltpu.VMEM((2, 4, ROWS, half), F32),
                pltpu.VMEM((2, ROWS, half), F32),
                pltpu.VMEM((2, ROWS, half), F32),
                pltpu.VMEM((2, ROWS, half), F32),
                pltpu.VMEM((2, 3, ROWS, half), F32),
                pltpu.VMEM((2, 3, ROWS, half), F32),
                pltpu.VMEM((2, ROWS, 2 * TILE), F32),
                pltpu.VMEM((2, ROWS, 2 * TILE), F32),
                pltpu.VMEM((2, 3, ROWS, half), F32),
                pltpu.VMEM((2, 3, ROWS, half), F32),
                pltpu.VMEM((2, ROWS, 2 * TILE), F32),
                pltpu.VMEM((2, ROWS, 2 * TILE), F32),
                pltpu.VMEM((2, ROWS, half), F32),
                pltpu.VMEM((ny, 5, ROWS, TILE), F32),
                pltpu.VMEM((ny, 5, ROWS, TILE), F32),
                pltpu.SemaphoreType.DMA((2,)),
                pltpu.SemaphoreType.DMA((2, 4)),
                pltpu.SemaphoreType.DMA((2, 4)),
                pltpu.SemaphoreType.DMA((ny,)),
                pltpu.SemaphoreType.DMA((ny,)),
            ],
            compiler_params=pltpu.CompilerParams(
                collective_id=0, has_side_effects=True, vmem_limit_bytes=24 * 2**20
            ),
        )(velocity, jnp.asarray(COLUMNS))
        return out.reshape(4 * ny, ROWS, TILE)

    return jax.shard_map(
        body, mesh=mesh, in_specs=(P("gy", "gx", None),), out_specs=P(None, "gx", "gy"), check_vma=False
    )
```

```python
import functools

import jax
import jax.numpy as jnp
import numpy as np
from jax import lax
from jax.experimental import pallas as pl
from jax.experimental.pallas import tpu as pltpu
from jax.sharding import PartitionSpec as P

PREDICT_FIRST = -1.586134342
UPDATE_FIRST = -0.05298011854
PREDICT_SECOND = 0.8829110762
UPDATE_SECOND = 0.4435068522
SCALE_LOW = 1.149604398
SCALE_HIGH = 1.0 / 1.149604398

MESH = pl.DeviceIdType.MESH
ROWS = 8
STEPS = (1, -1, 2, -2)
TILE = 128
F32 = jnp.float32


def lift_matrix(extent):
    table = np.eye(extent)
    s, r = table[0::2], table[1::2]
    r = r + PREDICT_FIRST * (s + np.roll(s, -1, 0))
    s = s + UPDATE_FIRST * (r + np.roll(r, 1, 0))
    r = r + PREDICT_SECOND * (s + np.roll(s, -1, 0))
    s = s + UPDATE_SECOND * (r + np.roll(r, 1, 0))
    out = np.empty((extent, extent))
    out[0::2], out[1::2] = s * SCALE_LOW, r * SCALE_HIGH
    return out


def row_operators():
    extent, mine = 128, 64
    first = lift_matrix(extent)
    second = lift_matrix(extent // 2) @ first[0::2]
    wide = np.zeros((extent, extent))
    wide[0::2] = second

    def block(table, step):
        start = mine + ROWS * step
        return table[start : start + ROWS, mine : mine + ROWS]

    return {step: block(first, step) for step in (-1, 0, 1)}, {step: block(wide, step) for step in (-2, -1, 0, 1, 2)}


def coefficient_columns():
    first, second = row_operators()
    columns, names = [], {}

    def add(name, column):
        if np.any(column != 0):
            names[name] = len(columns)
            columns.append(column)

    halo = first[1] + first[-1]
    assert not np.any((first[1] != 0) & (first[-1] != 0).any(axis=1, keepdims=True))
    even = np.arange(ROWS) // 2 * 2
    for j in range(ROWS):
        add(("own", j), first[0][:, j])
        add(("halo", j), halo[:, j])
        for step in (-1, 0, 1, 2):
            add((step, j), second[step][even, j])
    tail = np.zeros(ROWS)
    tail[4:] = second[-2][[4, 4, 6, 6], 0]
    add(("tail", 0), tail)
    table = np.zeros((ROWS, TILE), np.float32)
    table[:, : len(columns)] = np.stack(columns, 1)
    return table, names


COLUMNS, NAMES = coefficient_columns()


def lane_lift(s, r, stride):
    axis, length = s.ndim - 1, s.shape[-1]

    def after(a):
        return pltpu.roll(a, length - stride, axis)

    def before(a):
        return pltpu.roll(a, stride, axis)

    r = r + PREDICT_FIRST * (s + after(s))
    s = s + UPDATE_FIRST * (r + before(r))
    r = r + PREDICT_SECOND * (s + after(s))
    s = s + UPDATE_SECOND * (r + before(r))
    return s * SCALE_LOW, r * SCALE_HIGH


def swap(a, b, low, stride, axis):
    size = a.shape[axis]
    return jnp.where(low, a, pltpu.roll(b, stride, axis)), jnp.where(low, pltpu.roll(a, size - stride, axis), b)


def leading_lift(s, r):
    def after(a):
        return jnp.concatenate([a[1:], a[:1]], axis=0)

    def before(a):
        return jnp.concatenate([a[-1:], a[:-1]], axis=0)

    r = r + PREDICT_FIRST * (s + after(s))
    s = s + UPDATE_FIRST * (r + before(r))
    r = r + PREDICT_SECOND * (s + after(s))
    s = s + UPDATE_SECOND * (r + before(r))
    return s * SCALE_LOW, r * SCALE_HIGH


def kernel(nx, ny, v_hbm, table_hbm, out_ref, v_ref, table_ref, weights, y_one, y_two, own, own_two, far_two, near_two, go_right,
           go_left, go_right_two, go_left_two, from_left, from_right, from_left_two, from_right_two, tail_two, send, got,
           relay, relayed, in_sem, halo_send, halo_recv, send_sem, recv_sem, relay_send, relay_recv, go):
    gx, gy = lax.axis_index("gx"), lax.axis_index("gy")
    half = (gy // 2) % 2
    blocks = ny // 4
    width = 2 * blocks * TILE

    load = pltpu.make_async_copy(v_hbm, v_ref, in_sem.at[0])
    load.start()
    load_table = pltpu.make_async_copy(table_hbm, table_ref, in_sem.at[1])
    load_table.start()

    other = gy + 2 - 4 * half

    def wraps(step):
        return jnp.logical_or(gx + step < 0, gx + step >= nx)

    def beside(step):
        return (lax.rem(gx + step + nx, nx), gy)

    def nearest(step):
        return (lax.rem(gx + step + nx, nx), jnp.where(wraps(step), other, gy))

    def peer(side, j):
        block = lax.rem(gy // 4 + j // 2, blocks)
        core = lax.rem(gy + j, 2)
        return block, core, block * 4 + side * 2 + core

    barrier = pltpu.get_barrier_semaphore()
    far, near = 1 - half, half
    for step in STEPS:
        pl.semaphore_signal(barrier, inc=1, device_id=nearest(step), device_id_type=MESH)
    for j in range(1, 2 * blocks):
        pl.semaphore_signal(barrier, inc=1, device_id=(gx, peer(near, j)[2]), device_id_type=MESH)

    def greet_far(semaphore):
        for j in range(2 * blocks):
            pl.semaphore_signal(semaphore, inc=1, device_id=(gx, peer(far, j)[2]), device_id_type=MESH)

    for n in (0, 2):
        @pl.when(wraps(-STEPS[n]))
        def _():
            pl.semaphore_signal(barrier, inc=1, device_id=beside(-STEPS[n]), device_id_type=MESH)

    @pl.when(half == 0)
    def _():
        greet_far(barrier)

    load_table.wait()
    for at in range(len(NAMES)):
        weights[at] = jnp.broadcast_to(table_ref[:, at : at + 1], (ROWS, TILE))
    load.wait()

    lane = lax.broadcasted_iota(jnp.int32, (ROWS, TILE), 1)
    row = lax.broadcasted_iota(jnp.int32, (ROWS, TILE), 0)
    low_row = row < 4
    even_row = row % 2 == 0

    def low_lanes(stride):
        return jnp.concatenate([(lane // stride) % 2] * ny, axis=1) == 0

    lows = []
    for pair in range(2):
        s, r = swap(v_ref[2 * pair], v_ref[2 * pair + 1], low_lanes(1), 1, 1)
        s, r = lane_lift(s, r, 2)
        y_one[2 * pair] = s
        y_one[2 * pair + 1] = r
        lows.append(s)
    s, r = lane_lift(*swap(*lows, low_lanes(2), 2, 1), 4)
    y_two[0], y_two[1] = swap(s, r, low_lanes(2), 2, 1)

    def weigh(total, name, value):
        if name not in NAMES:
            return total
        term = weights[NAMES[name]] * value
        return term if total is None else total + term

    def down(value, k):
        return value if k % ROWS == 0 or isinstance(value, float) else pltpu.roll(value, k % ROWS, 0)

    def x_pass(side):
        @pl.loop(0, 2 * blocks)
        def _(p):
            tile = (p // 2) * 4 + side * 2 + p % 2
            lanes = pl.ds(pl.multiple_of(tile * TILE, TILE), TILE)
            here = pl.ds(pl.multiple_of(p * TILE, TILE), TILE)

            def spread(ref, z, j):
                return jnp.broadcast_to(ref[z, j : j + 1, lanes], (ROWS, TILE))

            mine, halos = [None] * 4, [None] * 4
            for j in range(ROWS):
                for z in range(4):
                    value = spread(y_one, z, j)
                    mine[z] = weigh(mine[z], ("own", j), value)
                    halos[z] = weigh(halos[z], ("halo", j), value)
            for z in range(4):
                own[side, z, :, here] = mine[z]
            for pair in range(2):
                a, b = halos[2 * pair], halos[2 * pair + 1]
                go_right[side, pair, :, here] = jnp.where(low_row, a, down(b, 4))
                go_left[side, pair, :, here] = jnp.where(low_row, down(a, 4), b)
            sums = {step: None for step in (-1, 0, 1, 2)}
            for j in range(ROWS):
                value = jnp.where(even_row, spread(y_two, 0, j), spread(y_two, 1, j))
                if j == 0:
                    near_two[side, :, here] = value
                for step in sums:
                    sums[step] = weigh(sums[step], (step, j), value)
            own_two[side, :, here] = sums[0]
            go_right[side, 2, :, here] = sums[1]
            go_left[side, 2, :, here] = sums[-1]
            far_two[side, :, here] = sums[2]

    wide_row = lax.broadcasted_iota(jnp.int32, (ROWS, 2 * TILE), 0)

    def pack_two(side):
        for source, target in ((far_two, go_right_two), (near_two, go_left_two)):
            packed = source[side, :, 0 : 2 * TILE]
            for block in range(1, blocks):
                value = down(source[side, :, block * 2 * TILE : (block + 1) * 2 * TILE], 2 * block)
                packed = jnp.where(wide_row // 2 == block, value, packed)
            target[side] = packed

    messages = (
        (go_right, from_left),
        (go_left, from_right),
        (go_right_two, from_left_two),
        (go_left_two, from_right_two),
    )

    def halo_copy(n, side, slot, device):
        return pltpu.make_async_remote_copy(
            src_ref=messages[n][0].at[side],
            dst_ref=messages[n][1].at[slot],
            send_sem=halo_send.at[side, n],
            recv_sem=halo_recv.at[slot, n],
            device_id=device,
            device_id_type=MESH,
        )

    def halo_out(n, side):
        step = STEPS[n]
        if side is near and step > 0:
            return halo_copy(n, side, side, beside(step))
        return halo_copy(n, side, side + jnp.where(wraps(step), 2, 0), nearest(step))

    def halo_in(n, side, wrapped):
        return halo_copy(n, side, side + (2 if wrapped else 0), beside(STEPS[n]))

    came = [wraps(-step) for step in STEPS]
    straight = [jnp.logical_not(flag) for flag in came]

    def kept(side):
        return straight if side is far else [gx >= 0, straight[1], gx >= 0, straight[3]]

    def only(flag, value):
        if isinstance(flag, bool):
            return value if flag else 0.0
        return jnp.where(flag, value, 0.0)

    def unpack_two(slot, keep):
        tail = NAMES[("tail", 0)]
        tails = jnp.broadcast_to(table_ref[:, tail : tail + 1], (ROWS, 2 * TILE))
        for block in range(blocks):
            head = jnp.where(wide_row < 2, down(from_left_two[slot], ROWS - 2 * block), 0.0)
            late = from_right_two[slot]
            late = jnp.where(wide_row < 6, down(late, 4 - 2 * block), down(late, 6 - 2 * block))
            tail_two[slot, :, block * 2 * TILE : (block + 1) * 2 * TILE] = only(keep[2], head) + only(keep[3], tails * late)

    def spread_rows(a, b):
        return [jnp.where(low_row, a, down(b, 4)), jnp.where(low_row, down(a, 4), b)]

    def halo_tiles(slot, keep, here):
        tiles = []
        for pair in range(2):
            tiles += spread_rows(only(keep[0], from_left[slot, pair, :, here]), only(keep[1], from_right[slot, pair, :, here]))
        a, b = only(keep[0], from_left[slot, 2, :, here]), only(keep[1], from_right[slot, 2, :, here])
        return tiles + [tail_two[slot, :, here] + (a + b)]

    def lanes_of(block, core):
        return pl.ds(pl.multiple_of((block * 2 + core) * TILE, TILE), TILE)

    def combine(side, block, core, target, slot):
        here = lanes_of(block, core)
        tiles = halo_tiles(side, kept(side), here)
        for n in range(4):
            target[slot, n] = own[side, n, :, here] + tiles[n]
        target[slot, 4] = own_two[side, :, here] + tiles[4]

    def tile_copy(tile):
        return pltpu.make_async_remote_copy(
            src_ref=send.at[tile],
            dst_ref=got.at[gy],
            send_sem=send_sem.at[tile],
            recv_sem=recv_sem.at[gy],
            device_id=(gx, tile),
            device_id_type=MESH,
        )

    def arrival(tile):
        return pltpu.make_async_remote_copy(
            src_ref=send.at[tile],
            dst_ref=got.at[tile],
            send_sem=send_sem.at[tile],
            recv_sem=recv_sem.at[tile],
            device_id=(gx, tile),
            device_id_type=MESH,
        )

    x_pass(far)
    pack_two(far)
    late_greetings = jnp.where(wraps(1), 2, jnp.where(wraps(2), 1, 0))
    pl.semaphore_wait(barrier, 4 + 2 * blocks - 1 + 2 * blocks * half + late_greetings)
    for n in range(4):
        halo_out(n, far).start()

    @pl.when(half == 1)
    def _():
        greet_far(go)

    x_pass(near)
    pack_two(near)
    for n in range(4):
        halo_out(n, near).start()

    def await_halos(side):
        for n in range(4):
            @pl.when(kept(side)[n])
            def _():
                halo_in(n, side, False).wait_recv()
        unpack_two(side, kept(side))

    def relay_copy(slot, tile, count):
        return pltpu.make_async_remote_copy(
            src_ref=relay.at[tile, pl.ds(0, count)],
            dst_ref=relayed.at[slot, pl.ds(0, count)],
            send_sem=relay_send.at[tile],
            recv_sem=relay_recv.at[slot],
            device_id=(gx, tile),
            device_id_type=MESH,
        )

    def at_ends(act, *ends):
        for low in ends:
            for place, count in ((0, 3), (1, 1)):
                @pl.when(gx == (place if low else nx - 1 - place))
                def _():
                    act(low, count)

    def pass_on(side, low, count):
        first = 1 if side is near else 0
        ones, twos = (from_left, 2) if low else (from_right, 3)
        slot = 2 + side

        def fill(block, core, target, place):
            here = lanes_of(block, core)
            value = tail_two[slot, :, here]
            if count == 3:
                target[place, 0] = value + ones[slot, 2, :, here]
                for pair in range(2):
                    target[place, 1 + pair] = ones[slot, pair, :, here]
            else:
                target[place, 0] = value

        for n in ((twos - 2, twos) if count == 3 else (twos,)):
            halo_in(n, side, True).wait_recv()
        unpack_two(slot, [None, None, low, not low])

        @pl.loop(first, 2 * blocks)
        def _(j):
            block, core, tile = peer(side, j)
            fill(block, core, relay, tile)
            relay_copy(gy, tile, count).start()

        if first:
            fill(gy // 4, lax.rem(gy, 2), relayed, gy)

    await_halos(far)

    @pl.loop(0, 2 * blocks)
    def _(j):
        block, core, tile = peer(far, j)
        combine(far, block, core, send, tile)

        @pl.when(half == 1)
        def _():
            tile_copy(tile).start()

    @pl.when(half == 1)
    def _():
        at_ends(functools.partial(pass_on, far), False)

    await_halos(near)

    @pl.loop(1, 2 * blocks)
    def _(j):
        block, core, tile = peer(near, j)
        combine(near, block, core, send, tile)
        tile_copy(tile).start()

    combine(near, gy // 4, lax.rem(gy, 2), got, gy)

    @pl.when(half == 0)
    def _():
        pl.semaphore_wait(go, 2 * blocks)

        @pl.loop(0, 2 * blocks)
        def _(j):
            tile_copy(peer(far, j)[2]).start()

        at_ends(functools.partial(pass_on, far), False)

    at_ends(functools.partial(pass_on, near), True, False)

    for n in range(4):
        halo_out(n, far).wait_send()
        halo_out(n, near).wait_send()

    @pl.loop(1, 2 * blocks)
    def _(j):
        arrival(peer(near, j)[2]).wait()

    @pl.loop(0, 2 * blocks)
    def _(j):
        arrival(peer(far, j)[2]).wait()

    def take_over(low, count):
        for side, first in ((near, 1),) if low else ((near, 1), (far, 0)):
            @pl.loop(first, 2 * blocks)
            def _(j):
                tile = peer(side, j)[2]
                relay_copy(tile, tile, count).wait()

        for side, back in ((near, far),) if low else ((near, far), (far, near)):
            @pl.loop(0, 2 * blocks)
            def _(j):
                tile, owner = peer(side, j)[2], peer(back, j)[2]
                if count == 3:
                    for pair in range(2):
                        value = relayed[tile, 1 + pair]
                        for n, rows in enumerate(spread_rows(value, 0.0) if low else spread_rows(0.0, value)):
                            got[owner, 2 * pair + n] += rows
                got[owner, 4] += relayed[tile, 0]

    at_ends(take_over, True, False)

    pairs = 2 * ny
    shape = (pairs, ROWS, TILE)
    wide = lax.broadcasted_iota(jnp.int32, (ny, ROWS, TILE), 2) % 2 == 0
    pairs_one = [swap(got[:, n], got[:, n + 1], wide, 1, 2) for n in (0, 2)]
    s, r = leading_lift(*(jnp.stack(both, axis=1).reshape(shape) for both in zip(*pairs_one)))
    slot = got[:, 4]
    under = pltpu.roll(slot, ROWS - 1, 1)

    def left(value):
        return pltpu.roll(value, TILE - 1, 2)

    even = jnp.stack([slot, under], axis=1).reshape(shape)
    odd = jnp.stack([left(slot), left(under)], axis=1).reshape(shape)
    coarse = leading_lift(even, odd)[0].reshape(ny, 2, ROWS, TILE)
    low, high = leading_lift(coarse[:, 0], coarse[:, 1])
    coarse = jnp.stack([low, high], axis=1).reshape(shape)
    corner = (lax.broadcasted_iota(jnp.int32, shape, 1) % 2 == 0) & (lax.broadcasted_iota(jnp.int32, shape, 2) % 2 == 0)
    out_ref[:, 0] = jnp.where(corner, coarse, s)
    out_ref[:, 1] = r


def solution(mesh):
    nx, ny = mesh.shape["gx"], mesh.shape["gy"]
    length = ny * TILE
    half = length // 2

    def body(velocity):
        out = pl.pallas_call(
            functools.partial(kernel, nx, ny),
            out_shape=jax.ShapeDtypeStruct((2 * ny, 2, ROWS, TILE), F32),
            in_specs=[pl.BlockSpec(memory_space=pl.ANY)] * 2,
            out_specs=pl.BlockSpec(memory_space=pltpu.VMEM),
            scratch_shapes=[
                pltpu.VMEM((4, ROWS, length), F32),
                pltpu.VMEM((ROWS, TILE), F32),
                pltpu.VMEM((len(NAMES), ROWS, TILE), F32),
                pltpu.VMEM((4, ROWS, length), F32),
                pltpu.VMEM((2, ROWS, length), F32),
                pltpu.VMEM((2, 4, ROWS, half), F32),
                pltpu.VMEM((2, ROWS, half), F32),
                pltpu.VMEM((2, ROWS, half), F32),
                pltpu.VMEM((2, ROWS, half), F32),
                pltpu.VMEM((2, 3, ROWS, half), F32),
                pltpu.VMEM((2, 3, ROWS, half), F32),
                pltpu.VMEM((2, ROWS, 2 * TILE), F32),
                pltpu.VMEM((2, ROWS, 2 * TILE), F32),
                pltpu.VMEM((4, 3, ROWS, half), F32),
                pltpu.VMEM((4, 3, ROWS, half), F32),
                pltpu.VMEM((4, ROWS, 2 * TILE), F32),
                pltpu.VMEM((4, ROWS, 2 * TILE), F32),
                pltpu.VMEM((4, ROWS, half), F32),
                pltpu.VMEM((ny, 5, ROWS, TILE), F32),
                pltpu.VMEM((ny, 5, ROWS, TILE), F32),
                pltpu.VMEM((ny, 3, ROWS, TILE), F32),
                pltpu.VMEM((ny, 3, ROWS, TILE), F32),
                pltpu.SemaphoreType.DMA((2,)),
                pltpu.SemaphoreType.DMA((2, 4)),
                pltpu.SemaphoreType.DMA((4, 4)),
                pltpu.SemaphoreType.DMA((ny,)),
                pltpu.SemaphoreType.DMA((ny,)),
                pltpu.SemaphoreType.DMA((ny,)),
                pltpu.SemaphoreType.DMA((ny,)),
                pltpu.SemaphoreType.REGULAR,
            ],
            compiler_params=pltpu.CompilerParams(collective_id=0, has_side_effects=True),
        )(velocity, jnp.asarray(COLUMNS))
        return out.reshape(4 * ny, ROWS, TILE)

    return jax.shard_map(
        body, mesh=mesh, in_specs=(P("gy", "gx", None),), out_specs=P(None, "gx", "gy"), check_vma=False
    )
```

```python
import functools

import jax
import jax.numpy as jnp
import numpy as np
from jax import lax
from jax.experimental import pallas as pl
from jax.experimental.pallas import tpu as pltpu
from jax.sharding import PartitionSpec as P

PREDICT_FIRST = -1.586134342
UPDATE_FIRST = -0.05298011854
PREDICT_SECOND = 0.8829110762
UPDATE_SECOND = 0.4435068522
SCALE_LOW = 1.149604398
SCALE_HIGH = 1.0 / 1.149604398

MESH = pl.DeviceIdType.MESH
ROWS = 8
STEPS = (1, -1, 2, -2)
TILE = 128
F32 = jnp.float32


def lift_matrix(extent):
    table = np.eye(extent)
    s, r = table[0::2], table[1::2]
    r = r + PREDICT_FIRST * (s + np.roll(s, -1, 0))
    s = s + UPDATE_FIRST * (r + np.roll(r, 1, 0))
    r = r + PREDICT_SECOND * (s + np.roll(s, -1, 0))
    s = s + UPDATE_SECOND * (r + np.roll(r, 1, 0))
    out = np.empty((extent, extent))
    out[0::2], out[1::2] = s * SCALE_LOW, r * SCALE_HIGH
    return out


LOW_TAPS = [float(tap) for tap in lift_matrix(32)[16, 16:21]]
HIGH_TAPS = [float(tap) for tap in lift_matrix(32)[17, 17:21]]


def row_operators():
    extent, mine = 128, 64
    first = lift_matrix(extent)
    second = lift_matrix(extent // 2) @ first[0::2]
    wide = np.zeros((extent, extent))
    wide[0::2] = second

    def block(table, step):
        start = mine + ROWS * step
        return table[start : start + ROWS, mine : mine + ROWS]

    return {step: block(first, step) for step in (-1, 0, 1)}, {step: block(wide, step) for step in (-2, -1, 0, 1, 2)}


def coefficient_columns():
    first, second = row_operators()
    columns, names = [], {}

    def add(name, column):
        if np.any(column != 0):
            names[name] = len(columns)
            columns.append(column)

    halo = first[1] + first[-1]
    assert not np.any((first[1] != 0) & (first[-1] != 0).any(axis=1, keepdims=True))
    even = np.arange(ROWS) // 2 * 2
    for j in range(ROWS):
        add(("own", j), first[0][:, j])
        add(("halo", j), halo[:, j])
        for step in (-1, 0, 1, 2):
            add((step, j), second[step][even, j])
    tail = np.zeros(ROWS)
    tail[4:] = second[-2][[4, 4, 6, 6], 0]
    add(("tail", 0), tail)
    table = np.zeros((ROWS, TILE), np.float32)
    table[:, : len(columns)] = np.stack(columns, 1)
    return table, names


COLUMNS, NAMES = coefficient_columns()


def lane_lift(s, r, stride):
    axis, length = s.ndim - 1, s.shape[-1]

    def at(a, pairs):
        return pltpu.roll(a, (-pairs * stride) % length, axis) if pairs else a

    low, high = LOW_TAPS, HIGH_TAPS
    s_next, s_last, r_next, r_last = at(s, 1), at(s, -1), at(r, 1), at(r, -1)
    s_after, s_before, r_before = at(s, 2), at(s, -2), at(r, -2)
    s_out = (low[0] * s + low[2] * (s_next + s_last)) + low[4] * (s_after + s_before)
    s_out = s_out + (low[1] * (r + r_last) + low[3] * (r_next + r_before))
    r_out = (high[0] * r + high[2] * (r_next + r_last)) + (high[1] * (s + s_next) + high[3] * (s_last + s_after))
    return s_out, r_out


def swap(a, b, low, stride, axis):
    size = a.shape[axis]
    return jnp.where(low, a, pltpu.roll(b, stride, axis)), jnp.where(low, pltpu.roll(a, size - stride, axis), b)


def leading_lift(s, r):
    def after(a):
        return jnp.concatenate([a[1:], a[:1]], axis=0)

    def before(a):
        return jnp.concatenate([a[-1:], a[:-1]], axis=0)

    r = r + PREDICT_FIRST * (s + after(s))
    s = s + UPDATE_FIRST * (r + before(r))
    r = r + PREDICT_SECOND * (s + after(s))
    s = s + UPDATE_SECOND * (r + before(r))
    return s * SCALE_LOW, r * SCALE_HIGH


def kernel(nx, ny, v_hbm, table_hbm, out_ref, v_ref, table_ref, weights, y_one, y_two, own, own_two, far_two, near_two, go_right,
           go_left, go_right_two, go_left_two, from_left, from_right, from_left_two, from_right_two, tail_two, send, got,
           relay, relayed, in_sem, halo_send, halo_recv, send_sem, recv_sem, relay_send, relay_recv, go, ready, join):
    gx, gy = lax.axis_index("gx"), lax.axis_index("gy")
    half = (gy // 2) % 2
    blocks = ny // 4
    width = 2 * blocks * TILE

    load = pltpu.make_async_copy(v_hbm, v_ref, in_sem.at[0])
    load.start()
    load_table = pltpu.make_async_copy(table_hbm, table_ref, in_sem.at[1])
    load_table.start()

    other = gy + 2 - 4 * half

    def wraps(step):
        return jnp.logical_or(gx + step < 0, gx + step >= nx)

    def beside(step):
        return (lax.rem(gx + step + nx, nx), gy)

    def nearest(step):
        return (lax.rem(gx + step + nx, nx), jnp.where(wraps(step), other, gy))

    def peer(side, j):
        block = lax.rem(gy // 4 + j // 2, blocks)
        core = lax.rem(gy + j, 2)
        return block, core, block * 4 + side * 2 + core

    barrier = pltpu.get_barrier_semaphore()
    far, near = 1 - half, half
    answered = [wraps(step) & (half == 0) if step > 0 else gx < 0 for step in STEPS]
    answers = [wraps(-step) & (half == 1) if step > 0 else gx < 0 for step in STEPS]
    for n in range(4):
        back = (1, 0, 3, 2)[n]

        @pl.when(jnp.logical_not(answers[back]))
        def _():
            pl.semaphore_signal(barrier, inc=1, device_id=nearest(STEPS[n]), device_id_type=MESH)
    column = gy // 4
    pl.semaphore_signal(barrier, inc=1, device_id=(gx, peer(near, 1)[2]), device_id_type=MESH)

    def signal_blocks(semaphore, flag):
        for block in range(blocks):
            @pl.when(flag(block))
            def _():
                for core in range(2):
                    tile = block * 4 + near * 2 + core
                    pl.semaphore_signal(semaphore, inc=1, device_id=(gx, tile), device_id_type=MESH)

    signal_blocks(barrier, lambda block: column < block)

    def greet_far(semaphore):
        for j in range(2 * blocks):
            pl.semaphore_signal(semaphore, inc=1, device_id=(gx, peer(far, j)[2]), device_id_type=MESH)

    heard = (half == 0)
    for n in range(4):
        @pl.when(wraps(-STEPS[n]) & (heard if STEPS[n] < 0 else gx >= 0))
        def _():
            pl.semaphore_signal(barrier, inc=1, device_id=beside(-STEPS[n]), device_id_type=MESH)

    @pl.when(half == 0)
    def _():
        greet_far(barrier)

    load_table.wait()
    for at in range(len(NAMES)):
        weights[at] = jnp.broadcast_to(table_ref[:, at : at + 1], (ROWS, TILE))
    load.wait()

    lane = lax.broadcasted_iota(jnp.int32, (ROWS, TILE), 1)
    row = lax.broadcasted_iota(jnp.int32, (ROWS, TILE), 0)
    low_row = row < 4
    even_row = row % 2 == 0

    def low_lanes(stride):
        return jnp.concatenate([(lane // stride) % 2] * ny, axis=1) == 0

    lows = []
    for pair in range(2):
        s, r = swap(v_ref[2 * pair], v_ref[2 * pair + 1], low_lanes(1), 1, 1)
        s, r = lane_lift(s, r, 2)
        y_one[2 * pair] = s
        y_one[2 * pair + 1] = r
        lows.append(s)
    s, r = lane_lift(*swap(*lows, low_lanes(2), 2, 1), 4)
    y_two[0], y_two[1] = swap(s, r, low_lanes(2), 2, 1)

    def weigh(total, name, value):
        if name not in NAMES:
            return total
        term = weights[NAMES[name]] * value
        return term if total is None else total + term

    def down(value, k):
        return value if k % ROWS == 0 or isinstance(value, float) else pltpu.roll(value, k % ROWS, 0)

    def x_pass(side):
        @pl.loop(0, 2 * blocks)
        def _(p):
            tile = (p // 2) * 4 + side * 2 + p % 2
            lanes = pl.ds(pl.multiple_of(tile * TILE, TILE), TILE)
            here = pl.ds(pl.multiple_of(p * TILE, TILE), TILE)

            def spread(ref, z, j):
                return jnp.broadcast_to(ref[z, j : j + 1, lanes], (ROWS, TILE))

            mine, halos = [None] * 4, [None] * 4
            for j in range(ROWS):
                for z in range(4):
                    value = spread(y_one, z, j)
                    mine[z] = weigh(mine[z], ("own", j), value)
                    halos[z] = weigh(halos[z], ("halo", j), value)
            for z in range(4):
                own[side, z, :, here] = mine[z]
            for pair in range(2):
                a, b = halos[2 * pair], halos[2 * pair + 1]
                go_right[side, pair, :, here] = jnp.where(low_row, a, down(b, 4))
                go_left[side, pair, :, here] = jnp.where(low_row, down(a, 4), b)
            sums = {step: None for step in (-1, 0, 1, 2)}
            for j in range(ROWS):
                value = jnp.where(even_row, spread(y_two, 0, j), spread(y_two, 1, j))
                if j == 0:
                    near_two[side, :, here] = value
                for step in sums:
                    sums[step] = weigh(sums[step], (step, j), value)
            own_two[side, :, here] = sums[0]
            go_right[side, 2, :, here] = sums[1]
            go_left[side, 2, :, here] = sums[-1]
            far_two[side, :, here] = sums[2]

    wide_row = lax.broadcasted_iota(jnp.int32, (ROWS, 2 * TILE), 0)

    def pack_two(side):
        for source, target in ((far_two, go_right_two), (near_two, go_left_two)):
            packed = source[side, :, 0 : 2 * TILE]
            for block in range(1, blocks):
                value = down(source[side, :, block * 2 * TILE : (block + 1) * 2 * TILE], 2 * block)
                packed = jnp.where(wide_row // 2 == block, value, packed)
            target[side] = packed

    messages = (
        (go_right, from_left),
        (go_left, from_right),
        (go_right_two, from_left_two),
        (go_left_two, from_right_two),
    )

    def halo_copy(n, side, slot, device, block=None):
        source, target = messages[n][0].at[side], messages[n][1].at[slot]
        at = n
        if block is not None:
            lanes = pl.ds(pl.multiple_of(block * 2 * TILE, 2 * TILE), 2 * TILE)
            source, target = source.at[:, :, lanes], target.at[:, :, lanes]
            at = 4 + n * blocks + block
        return pltpu.make_async_remote_copy(
            src_ref=source,
            dst_ref=target,
            send_sem=halo_send.at[side, at],
            recv_sem=halo_recv.at[slot, at],
            device_id=device,
            device_id_type=MESH,
        )

    def halo_out(n, side, block=None):
        step = STEPS[n]
        if side is near:
            by_other = wraps(step) & (half == 1) & (step < 0)
            gx_to, gy_to = beside(step)
            return halo_copy(n, side, jnp.where(by_other, 3, side), (gx_to, jnp.where(by_other, other, gy_to)), block)
        return halo_copy(n, side, jnp.where(wraps(step), 2, side), nearest(step), block)

    def halo_in(n, side, block=None):
        return halo_copy(n, side, side, beside(STEPS[n]), block)

    def wrapped_in(n, side, block=None):
        return halo_copy(n, side, 2 if side is near else 3, beside(STEPS[n]), block)

    def block_from_here(i):
        return lax.rem(gy // 4 + i, blocks)

    came = [wraps(-step) for step in STEPS]
    straight = [jnp.logical_not(flag) for flag in came]

    def kept(side):
        return straight if side is far else [True, straight[1] | (half == 0), True, straight[3] | (half == 0)]

    def only(flag, value):
        if isinstance(flag, bool):
            return value if flag else 0.0
        return jnp.where(flag, value, 0.0)

    def unpack_two(slot, keep):
        tail = NAMES[("tail", 0)]
        tails = jnp.broadcast_to(table_ref[:, tail : tail + 1], (ROWS, 2 * TILE))
        for block in range(blocks):
            head = jnp.where(wide_row < 2, down(from_left_two[slot], ROWS - 2 * block), 0.0)
            late = from_right_two[slot]
            late = jnp.where(wide_row < 6, down(late, 4 - 2 * block), down(late, 6 - 2 * block))
            tail_two[slot, :, block * 2 * TILE : (block + 1) * 2 * TILE] = only(keep[2], head) + only(keep[3], tails * late)

    def spread_rows(a, b):
        return [jnp.where(low_row, a, down(b, 4)), jnp.where(low_row, down(a, 4), b)]

    def halo_tiles(slot, keep, here):
        tiles = []
        for pair in range(2):
            tiles += spread_rows(only(keep[0], from_left[slot, pair, :, here]), only(keep[1], from_right[slot, pair, :, here]))
        a, b = only(keep[0], from_left[slot, 2, :, here]), only(keep[1], from_right[slot, 2, :, here])
        return tiles + [tail_two[slot, :, here] + (a + b)]

    def lanes_of(block, core):
        return pl.ds(pl.multiple_of((block * 2 + core) * TILE, TILE), TILE)

    def combine(side, block, core, target, slot):
        here = lanes_of(block, core)
        tiles = halo_tiles(side, kept(side), here)
        for n in range(4):
            target[slot, n] = own[side, n, :, here] + tiles[n]
        target[slot, 4] = own_two[side, :, here] + tiles[4]

    def tile_copy(tile):
        return pltpu.make_async_remote_copy(
            src_ref=send.at[tile],
            dst_ref=got.at[gy],
            send_sem=send_sem.at[tile],
            recv_sem=recv_sem.at[gy],
            device_id=(gx, tile),
            device_id_type=MESH,
        )

    def arrival(tile):
        return pltpu.make_async_remote_copy(
            src_ref=send.at[tile],
            dst_ref=got.at[tile],
            send_sem=send_sem.at[tile],
            recv_sem=recv_sem.at[tile],
            device_id=(gx, tile),
            device_id_type=MESH,
        )

    x_pass(far)
    pack_two(far)
    late_greetings = jnp.where(wraps(1), 2, jnp.where(wraps(2), 1, 0)) * half
    late_greetings += jnp.where(wraps(-1), 2, jnp.where(wraps(-2), 1, 0)) * jnp.where(heard, 1, 0)
    near_first = (half == 0) | wraps(8)

    @pl.when(near_first)
    def _():
        x_pass(near)
        pack_two(near)

    pl.semaphore_wait(barrier, 5 + 2 * column + 2 * blocks * half + late_greetings)

    @pl.when(half == 1)
    def _():
        greet_far(go.at[column])

    def send_far_halos(n, condition):
        @pl.when(condition)
        def _():
            if n > 1:
                halo_out(n, far).start()
            else:
                @pl.loop(0, blocks)
                def _(i):
                    halo_out(n, far, block_from_here(i)).start()

    around = [wraps(step) & (heard if step < 0 else gx >= 0) for step in STEPS]
    for n in (2, 0):
        send_far_halos(n, around[n] & jnp.logical_not(answered[n]))
    for n in range(4):
        @pl.when(around[n])
        def _():
            halo_out(n, near).start()
    for n in (2, 3, 0, 1):
        send_far_halos(n, jnp.logical_not(around[n]) if STEPS[n] > 0 else gx >= 0)

    @pl.when(half == 1)
    def _():
        for n in (0, 2):
            @pl.when(answers[n])
            def _():
                pl.semaphore_signal(ready.at[n], inc=1, device_id=nearest(-STEPS[n]), device_id_type=MESH)

    signal_blocks(join, lambda block: column > block)

    @pl.when(jnp.logical_not(near_first))
    def _():
        x_pass(near)
        pack_two(near)

    late_near = (half == 1) & (lax.rem(gx, 4) == 0) & (gx < 24)

    def send_near_halos(flag):
        for n in range(4):
            @pl.when(flag & (jnp.logical_not(wraps(STEPS[n])) | ((half == 1) & (STEPS[n] < 0))))
            def _():
                halo_out(n, near).start()

    send_near_halos(jnp.logical_not(late_near) | wraps(-2))

    def await_halos(numbers, side, block=None):
        for n in numbers:
            @pl.when(kept(side)[n])
            def _():
                halo_in(n, side, block).wait_recv()

    def relay_copy(slot, tile, count):
        return pltpu.make_async_remote_copy(
            src_ref=relay.at[tile, pl.ds(0, count)],
            dst_ref=relayed.at[slot, pl.ds(0, count)],
            send_sem=relay_send.at[tile],
            recv_sem=relay_recv.at[slot],
            device_id=(gx, tile),
            device_id_type=MESH,
        )

    def at_ends(act, *ends):
        for low in ends:
            for place, count in ((0, 3), (1, 1)):
                @pl.when(gx == (place if low else nx - 1 - place))
                def _():
                    act(low, count)

    def pass_on(side, low, count):
        ones, twos = (from_left, 2) if low else (from_right, 3)
        slot = 2 if side is near else 3

        def fill(block, core, target, place):
            here = lanes_of(block, core)
            value = tail_two[slot, :, here]
            if count == 3:
                target[place, 0] = value + ones[slot, 2, :, here]
                for pair in range(2):
                    target[place, 1 + pair] = ones[slot, pair, :, here]
            else:
                target[place, 0] = value

        wrapped_in(twos, side).wait_recv()
        if count == 3 and side is far:
            wrapped_in(twos - 2, side).wait_recv()
        elif count == 3:
            for block in range(blocks):
                wrapped_in(twos - 2, side, block).wait_recv()
        unpack_two(slot, [None, None, low, not low])

        @pl.loop(1 if side is near else 0, 2 * blocks)
        def _(j):
            block, core, tile = peer(side, j)
            fill(block, core, relay, tile)
            relay_copy(gy, tile, count).start()

        if side is near:
            fill(gy // 4, lax.rem(gy, 2), relayed, gy)

    await_halos((2, 3), far)
    unpack_two(far, kept(far))

    @pl.loop(0, blocks)
    def _(i):
        await_halos((0, 1), far, block_from_here(i))
        for j in range(2):
            block, core, tile = peer(far, 2 * i + j)
            combine(far, block, core, send, tile)

            @pl.when(half == 1)
            def _():
                tile_copy(tile).start()

    send_near_halos(late_near & jnp.logical_not(wraps(-2)))

    for n in (0, 2):
        @pl.when(answered[n])
        def _():
            pl.semaphore_wait(ready.at[n], 1)
        send_far_halos(n, answered[n])

    @pl.when(half == 0)
    def _():
        @pl.loop(0, blocks)
        def _(block):
            pl.semaphore_wait(go.at[block], 2)
            for core in range(2):
                tile_copy(block * 4 + far * 2 + core).start()

        at_ends(functools.partial(pass_on, far), False)

    await_halos(range(4), near)
    unpack_two(near, kept(near))
    @pl.when(column < blocks - 1)
    def _():
        pl.semaphore_wait(join, 2 * (blocks - 1 - column))

    @pl.loop(1, 2 * blocks)
    def _(j):
        block, core, tile = peer(near, j)
        combine(near, block, core, send, tile)
        tile_copy(tile).start()

    combine(near, gy // 4, lax.rem(gy, 2), got, gy)

    at_ends(functools.partial(pass_on, near), True, False)


    @pl.loop(1, 2 * blocks)
    def _(j):
        arrival(peer(near, j)[2]).wait_recv()

    @pl.loop(0, 2 * blocks)
    def _(j):
        arrival(peer(far, j)[2]).wait_recv()

    def take_over(low, count):
        def take(side, first, back):
            @pl.loop(first, 2 * blocks)
            def _(j):
                tile = peer(side, j)[2]
                relay_copy(tile, tile, count).wait_recv()

            @pl.loop(0, 2 * blocks)
            def _(j):
                tile, owner = peer(side, j)[2], peer(back, j)[2]
                if count == 3:
                    for pair in range(2):
                        value = relayed[tile, 1 + pair]
                        for n, rows in enumerate(spread_rows(value, 0.0) if low else spread_rows(0.0, value)):
                            got[owner, 2 * pair + n] += rows
                got[owner, 4] += relayed[tile, 0]

        take(near, 1, far)
        if not low:
            @pl.when(half == 1)
            def _():
                take(far, 0, near)

    at_ends(take_over, True, False)

    pairs = 2 * ny
    shape = (pairs, ROWS, TILE)
    wide = lax.broadcasted_iota(jnp.int32, (ny, ROWS, TILE), 2) % 2 == 0
    pairs_one = [swap(got[:, n], got[:, n + 1], wide, 1, 2) for n in (0, 2)]
    s, r = leading_lift(*(jnp.stack(both, axis=1).reshape(shape) for both in zip(*pairs_one)))
    slot = got[:, 4]
    under = pltpu.roll(slot, ROWS - 1, 1)

    def left(value):
        return pltpu.roll(value, TILE - 1, 2)

    even = jnp.stack([slot, under], axis=1).reshape(shape)
    odd = jnp.stack([left(slot), left(under)], axis=1).reshape(shape)
    coarse = leading_lift(even, odd)[0].reshape(ny, 2, ROWS, TILE)
    low, high = leading_lift(coarse[:, 0], coarse[:, 1])
    coarse = jnp.stack([low, high], axis=1).reshape(shape)
    corner = (lax.broadcasted_iota(jnp.int32, shape, 1) % 2 == 0) & (lax.broadcasted_iota(jnp.int32, shape, 2) % 2 == 0)
    out_ref[:, 0] = jnp.where(corner, coarse, s)
    out_ref[:, 1] = r

    for n in range(4):
        halo_out(n, near).wait_send()
    for n in (2, 3):
        halo_out(n, far).wait_send()

    @pl.loop(0, blocks)
    def _(i):
        for n in (0, 1):
            halo_out(n, far, block_from_here(i)).wait_send()

    @pl.loop(1, 2 * blocks)
    def _(j):
        tile_copy(peer(near, j)[2]).wait_send()

    @pl.loop(0, 2 * blocks)
    def _(j):
        tile_copy(peer(far, j)[2]).wait_send()

    def drain(low, count):
        @pl.loop(1, 2 * blocks)
        def _(j):
            relay_copy(gy, peer(near, j)[2], count).wait_send()

        if not low:
            @pl.when(half == 0)
            def _():
                @pl.loop(0, 2 * blocks)
                def _(j):
                    relay_copy(gy, peer(far, j)[2], count).wait_send()

    at_ends(drain, True, False)


def solution(mesh):
    nx, ny = mesh.shape["gx"], mesh.shape["gy"]
    length = ny * TILE
    half = length // 2

    def body(velocity):
        out = pl.pallas_call(
            functools.partial(kernel, nx, ny),
            out_shape=jax.ShapeDtypeStruct((2 * ny, 2, ROWS, TILE), F32),
            in_specs=[pl.BlockSpec(memory_space=pl.ANY)] * 2,
            out_specs=pl.BlockSpec(memory_space=pltpu.VMEM),
            scratch_shapes=[
                pltpu.VMEM((4, ROWS, length), F32),
                pltpu.VMEM((ROWS, TILE), F32),
                pltpu.VMEM((len(NAMES), ROWS, TILE), F32),
                pltpu.VMEM((4, ROWS, length), F32),
                pltpu.VMEM((2, ROWS, length), F32),
                pltpu.VMEM((2, 4, ROWS, half), F32),
                pltpu.VMEM((2, ROWS, half), F32),
                pltpu.VMEM((2, ROWS, half), F32),
                pltpu.VMEM((2, ROWS, half), F32),
                pltpu.VMEM((2, 3, ROWS, half), F32),
                pltpu.VMEM((2, 3, ROWS, half), F32),
                pltpu.VMEM((2, ROWS, 2 * TILE), F32),
                pltpu.VMEM((2, ROWS, 2 * TILE), F32),
                pltpu.VMEM((4, 3, ROWS, half), F32),
                pltpu.VMEM((4, 3, ROWS, half), F32),
                pltpu.VMEM((4, ROWS, 2 * TILE), F32),
                pltpu.VMEM((4, ROWS, 2 * TILE), F32),
                pltpu.VMEM((4, ROWS, half), F32),
                pltpu.VMEM((ny, 5, ROWS, TILE), F32),
                pltpu.VMEM((ny, 5, ROWS, TILE), F32),
                pltpu.VMEM((ny, 3, ROWS, TILE), F32),
                pltpu.VMEM((ny, 3, ROWS, TILE), F32),
                pltpu.SemaphoreType.DMA((2,)),
                pltpu.SemaphoreType.DMA((2, 4 + ny // 2)),
                pltpu.SemaphoreType.DMA((4, 4 + ny // 2)),
                pltpu.SemaphoreType.DMA((ny,)),
                pltpu.SemaphoreType.DMA((ny,)),
                pltpu.SemaphoreType.DMA((ny,)),
                pltpu.SemaphoreType.DMA((ny,)),
                pltpu.SemaphoreType.REGULAR((ny // 4,)),
                pltpu.SemaphoreType.REGULAR((4,)),
                pltpu.SemaphoreType.REGULAR,
            ],
            compiler_params=pltpu.CompilerParams(collective_id=0, has_side_effects=True),
        )(velocity, jnp.asarray(COLUMNS))
        return out.reshape(4 * ny, ROWS, TILE)

    return jax.shard_map(
        body, mesh=mesh, in_specs=(P("gy", "gx", None),), out_specs=P(None, "gx", "gy"), check_vma=False
    )
```

```python
import functools

import jax
import jax.numpy as jnp
import numpy as np
from jax import lax
from jax.experimental import pallas as pl
from jax.experimental.pallas import tpu as pltpu
from jax.sharding import PartitionSpec as P

PREDICT_FIRST = -1.586134342
UPDATE_FIRST = -0.05298011854
PREDICT_SECOND = 0.8829110762
UPDATE_SECOND = 0.4435068522
SCALE_LOW = 1.149604398
SCALE_HIGH = 1.0 / 1.149604398

MESH = pl.DeviceIdType.MESH
ROWS = 8
STEPS = (1, -1, 2, -2)
TILE = 128
F32 = jnp.float32


def lift_matrix(extent):
    table = np.eye(extent)
    s, r = table[0::2], table[1::2]
    r = r + PREDICT_FIRST * (s + np.roll(s, -1, 0))
    s = s + UPDATE_FIRST * (r + np.roll(r, 1, 0))
    r = r + PREDICT_SECOND * (s + np.roll(s, -1, 0))
    s = s + UPDATE_SECOND * (r + np.roll(r, 1, 0))
    out = np.empty((extent, extent))
    out[0::2], out[1::2] = s * SCALE_LOW, r * SCALE_HIGH
    return out


LOW_TAPS = [float(tap) for tap in lift_matrix(32)[16, 16:21]]
HIGH_TAPS = [float(tap) for tap in lift_matrix(32)[17, 17:21]]


def row_operators():
    extent, mine = 128, 64
    first = lift_matrix(extent)
    second = lift_matrix(extent // 2) @ first[0::2]
    wide = np.zeros((extent, extent))
    wide[0::2] = second

    def block(table, step):
        start = mine + ROWS * step
        return table[start : start + ROWS, mine : mine + ROWS]

    return {step: block(first, step) for step in (-1, 0, 1)}, {step: block(wide, step) for step in (-2, -1, 0, 1, 2)}


def coefficient_columns():
    first, second = row_operators()
    columns, names = [], {}

    def add(name, column):
        if np.any(column != 0):
            names[name] = len(columns)
            columns.append(column)

    halo = first[1] + first[-1]
    assert not np.any((first[1] != 0) & (first[-1] != 0).any(axis=1, keepdims=True))
    even = np.arange(ROWS) // 2 * 2
    for j in range(ROWS):
        add(("own", j), first[0][:, j])
        add(("halo", j), halo[:, j])
        for step in (-1, 0, 1, 2):
            add((step, j), second[step][even, j])
    tail = np.zeros(ROWS)
    tail[4:] = second[-2][[4, 4, 6, 6], 0]
    add(("tail", 0), tail)
    table = np.zeros((ROWS, TILE), np.float32)
    table[:, : len(columns)] = np.stack(columns, 1)
    return table, names


COLUMNS, NAMES = coefficient_columns()


def lane_lift(s, r, stride):
    axis, length = s.ndim - 1, s.shape[-1]

    def at(a, pairs):
        return pltpu.roll(a, (-pairs * stride) % length, axis) if pairs else a

    low, high = LOW_TAPS, HIGH_TAPS
    s_next, s_last, r_next, r_last = at(s, 1), at(s, -1), at(r, 1), at(r, -1)
    s_after, s_before, r_before = at(s, 2), at(s, -2), at(r, -2)
    s_out = (low[0] * s + low[2] * (s_next + s_last)) + low[4] * (s_after + s_before)
    s_out = s_out + (low[1] * (r + r_last) + low[3] * (r_next + r_before))
    r_out = (high[0] * r + high[2] * (r_next + r_last)) + (high[1] * (s + s_next) + high[3] * (s_last + s_after))
    return s_out, r_out


def swap(a, b, low, stride, axis):
    size = a.shape[axis]
    return jnp.where(low, a, pltpu.roll(b, stride, axis)), jnp.where(low, pltpu.roll(a, size - stride, axis), b)


def leading_lift(s, r):
    def after(a):
        return jnp.concatenate([a[1:], a[:1]], axis=0)

    def before(a):
        return jnp.concatenate([a[-1:], a[:-1]], axis=0)

    r = r + PREDICT_FIRST * (s + after(s))
    s = s + UPDATE_FIRST * (r + before(r))
    r = r + PREDICT_SECOND * (s + after(s))
    s = s + UPDATE_SECOND * (r + before(r))
    return s * SCALE_LOW, r * SCALE_HIGH


def kernel(nx, ny, v_hbm, table_hbm, out_ref, v_ref, table_ref, weights, y_one, y_two, own, own_two, far_two, near_two, go_right,
           go_left, go_right_two, go_left_two, from_left, from_right, from_left_two, from_right_two, tail_two, send, got,
           relay, relayed, in_sem, halo_send, halo_recv, send_sem, recv_sem, relay_send, relay_recv, go, ready, join):
    gx, gy = lax.axis_index("gx"), lax.axis_index("gy")
    half = (gy // 2) % 2
    blocks = ny // 4
    width = 2 * blocks * TILE

    load = pltpu.make_async_copy(v_hbm, v_ref, in_sem.at[0])
    load.start()
    load_table = pltpu.make_async_copy(table_hbm, table_ref, in_sem.at[1])
    load_table.start()

    other = gy + 2 - 4 * half

    def wraps(step):
        return jnp.logical_or(gx + step < 0, gx + step >= nx)

    def beside(step):
        return (lax.rem(gx + step + nx, nx), gy)

    def nearest(step):
        return (lax.rem(gx + step + nx, nx), jnp.where(wraps(step), other, gy))

    def peer(side, j):
        block = lax.rem(gy // 4 + j // 2, blocks)
        core = lax.rem(gy + j, 2)
        return block, core, block * 4 + side * 2 + core

    barrier = pltpu.get_barrier_semaphore()
    far, near = 1 - half, half
    answered = [wraps(step) & (half == 0) if step > 0 else gx < 0 for step in STEPS]
    answers = [wraps(-step) & (half == 1) if step > 0 else gx < 0 for step in STEPS]
    for n in range(4):
        back = (1, 0, 3, 2)[n]

        @pl.when(jnp.logical_not(answers[back]))
        def _():
            pl.semaphore_signal(barrier, inc=1, device_id=nearest(STEPS[n]), device_id_type=MESH)
    column = gy // 4
    pl.semaphore_signal(barrier, inc=1, device_id=(gx, peer(near, 1)[2]), device_id_type=MESH)

    def signal_blocks(semaphore, flag):
        for block in range(blocks):
            @pl.when(flag(block))
            def _():
                for core in range(2):
                    tile = block * 4 + near * 2 + core
                    pl.semaphore_signal(semaphore, inc=1, device_id=(gx, tile), device_id_type=MESH)

    signal_blocks(barrier, lambda block: column < block)

    def greet_far(semaphore):
        for j in range(2 * blocks):
            pl.semaphore_signal(semaphore, inc=1, device_id=(gx, peer(far, j)[2]), device_id_type=MESH)

    heard = (half == 0)
    for n in range(4):
        @pl.when(wraps(-STEPS[n]) & (heard if STEPS[n] < 0 else gx >= 0))
        def _():
            pl.semaphore_signal(barrier, inc=1, device_id=beside(-STEPS[n]), device_id_type=MESH)

    @pl.when(half == 0)
    def _():
        greet_far(barrier)

    load_table.wait()
    for at in range(len(NAMES)):
        weights[at] = jnp.broadcast_to(table_ref[:, at : at + 1], (ROWS, TILE))
    load.wait()

    lane = lax.broadcasted_iota(jnp.int32, (ROWS, TILE), 1)
    row = lax.broadcasted_iota(jnp.int32, (ROWS, TILE), 0)
    low_row = row < 4
    even_row = row % 2 == 0

    def low_lanes(stride):
        return jnp.concatenate([(lane // stride) % 2] * ny, axis=1) == 0

    lows = []
    for pair in range(2):
        s, r = swap(v_ref[2 * pair], v_ref[2 * pair + 1], low_lanes(1), 1, 1)
        s, r = lane_lift(s, r, 2)
        y_one[2 * pair] = s
        y_one[2 * pair + 1] = r
        lows.append(s)
    s, r = lane_lift(*swap(*lows, low_lanes(2), 2, 1), 4)
    y_two[0], y_two[1] = swap(s, r, low_lanes(2), 2, 1)

    def weigh(total, name, value):
        if name not in NAMES:
            return total
        term = weights[NAMES[name]] * value
        return term if total is None else total + term

    def down(value, k):
        return value if k % ROWS == 0 or isinstance(value, float) else pltpu.roll(value, k % ROWS, 0)

    def x_pass(side):
        @pl.loop(0, 2 * blocks)
        def _(p):
            tile = (p // 2) * 4 + side * 2 + p % 2
            lanes = pl.ds(pl.multiple_of(tile * TILE, TILE), TILE)
            here = pl.ds(pl.multiple_of(p * TILE, TILE), TILE)

            def spread(ref, z, j):
                return jnp.broadcast_to(ref[z, j : j + 1, lanes], (ROWS, TILE))

            mine, halos = [None] * 4, [None] * 4
            for j in range(ROWS):
                for z in range(4):
                    value = spread(y_one, z, j)
                    mine[z] = weigh(mine[z], ("own", j), value)
                    halos[z] = weigh(halos[z], ("halo", j), value)
            for z in range(4):
                own[side, z, :, here] = mine[z]
            for pair in range(2):
                a, b = halos[2 * pair], halos[2 * pair + 1]
                go_right[side, pair, :, here] = jnp.where(low_row, a, down(b, 4))
                go_left[side, pair, :, here] = jnp.where(low_row, down(a, 4), b)
            sums = {step: None for step in (-1, 0, 1, 2)}
            for j in range(ROWS):
                value = jnp.where(even_row, spread(y_two, 0, j), spread(y_two, 1, j))
                if j == 0:
                    near_two[side, :, here] = value
                for step in sums:
                    sums[step] = weigh(sums[step], (step, j), value)
            own_two[side, :, here] = sums[0]
            go_right[side, 2, :, here] = sums[1]
            go_left[side, 2, :, here] = sums[-1]
            far_two[side, :, here] = sums[2]

    wide_row = lax.broadcasted_iota(jnp.int32, (ROWS, 2 * TILE), 0)

    def pack_two(side):
        for source, target in ((far_two, go_right_two), (near_two, go_left_two)):
            packed = source[side, :, 0 : 2 * TILE]
            for block in range(1, blocks):
                value = down(source[side, :, block * 2 * TILE : (block + 1) * 2 * TILE], 2 * block)
                packed = jnp.where(wide_row // 2 == block, value, packed)
            target[side] = packed

    messages = (
        (go_right, from_left),
        (go_left, from_right),
        (go_right_two, from_left_two),
        (go_left_two, from_right_two),
    )

    def halo_copy(n, side, slot, device, block=None):
        source, target = messages[n][0].at[side], messages[n][1].at[slot]
        at = n
        if block is not None:
            lanes = pl.ds(pl.multiple_of(block * 2 * TILE, 2 * TILE), 2 * TILE)
            source, target = source.at[:, :, lanes], target.at[:, :, lanes]
            at = 4 + n * blocks + block
        return pltpu.make_async_remote_copy(
            src_ref=source,
            dst_ref=target,
            send_sem=halo_send.at[side, at],
            recv_sem=halo_recv.at[slot, at],
            device_id=device,
            device_id_type=MESH,
        )

    def halo_out(n, side, block=None):
        step = STEPS[n]
        if side is near:
            by_other = wraps(step) & (half == 1) & (step < 0)
            gx_to, gy_to = beside(step)
            return halo_copy(n, side, jnp.where(by_other, 3, side), (gx_to, jnp.where(by_other, other, gy_to)), block)
        return halo_copy(n, side, jnp.where(wraps(step), 2, side), nearest(step), block)

    def halo_in(n, side, block=None):
        return halo_copy(n, side, side, beside(STEPS[n]), block)

    def wrapped_in(n, side, block=None):
        return halo_copy(n, side, 2 if side is near else 3, beside(STEPS[n]), block)

    def block_from_here(i):
        return lax.rem(gy // 4 + i, blocks)

    came = [wraps(-step) for step in STEPS]
    straight = [jnp.logical_not(flag) for flag in came]

    def kept(side):
        return straight if side is far else [True, straight[1] | (half == 0), True, straight[3] | (half == 0)]

    def only(flag, value):
        if isinstance(flag, bool):
            return value if flag else 0.0
        return jnp.where(flag, value, 0.0)

    def unpack_two(slot, keep):
        tail = NAMES[("tail", 0)]
        tails = jnp.broadcast_to(table_ref[:, tail : tail + 1], (ROWS, 2 * TILE))
        for block in range(blocks):
            head = jnp.where(wide_row < 2, down(from_left_two[slot], ROWS - 2 * block), 0.0)
            late = from_right_two[slot]
            late = jnp.where(wide_row < 6, down(late, 4 - 2 * block), down(late, 6 - 2 * block))
            tail_two[slot, :, block * 2 * TILE : (block + 1) * 2 * TILE] = only(keep[2], head) + only(keep[3], tails * late)

    def spread_rows(a, b):
        return [jnp.where(low_row, a, down(b, 4)), jnp.where(low_row, down(a, 4), b)]

    def halo_tiles(slot, keep, here):
        tiles = []
        for pair in range(2):
            tiles += spread_rows(only(keep[0], from_left[slot, pair, :, here]), only(keep[1], from_right[slot, pair, :, here]))
        a, b = only(keep[0], from_left[slot, 2, :, here]), only(keep[1], from_right[slot, 2, :, here])
        return tiles + [tail_two[slot, :, here] + (a + b)]

    def lanes_of(block, core):
        return pl.ds(pl.multiple_of((block * 2 + core) * TILE, TILE), TILE)

    def combine(side, block, core, target, slot):
        here = lanes_of(block, core)
        tiles = halo_tiles(side, kept(side), here)
        for n in range(4):
            target[slot, n] = own[side, n, :, here] + tiles[n]
        target[slot, 4] = own_two[side, :, here] + tiles[4]

    def tile_copy(tile):
        return pltpu.make_async_remote_copy(
            src_ref=send.at[tile],
            dst_ref=got.at[gy],
            send_sem=send_sem.at[tile],
            recv_sem=recv_sem.at[gy],
            device_id=(gx, tile),
            device_id_type=MESH,
        )

    def arrival(tile):
        return pltpu.make_async_remote_copy(
            src_ref=send.at[tile],
            dst_ref=got.at[tile],
            send_sem=send_sem.at[tile],
            recv_sem=recv_sem.at[tile],
            device_id=(gx, tile),
            device_id_type=MESH,
        )

    x_pass(far)
    pack_two(far)
    late_greetings = jnp.where(wraps(1), 2, jnp.where(wraps(2), 1, 0)) * half
    late_greetings += jnp.where(wraps(-1), 2, jnp.where(wraps(-2), 1, 0)) * jnp.where(heard, 1, 0)
    near_first = (half == 0) | wraps(8)

    @pl.when(near_first)
    def _():
        x_pass(near)
        pack_two(near)

    pl.semaphore_wait(barrier, 5 + 2 * column + 2 * blocks * half + late_greetings)

    @pl.when(half == 1)
    def _():
        greet_far(go.at[column])

    def send_far_halos(n, condition):
        @pl.when(condition)
        def _():
            if n > 1:
                halo_out(n, far).start()
            else:
                @pl.loop(0, blocks)
                def _(i):
                    halo_out(n, far, block_from_here(i)).start()

    around = [wraps(step) & (heard if step < 0 else gx >= 0) for step in STEPS]
    for n in (2, 0):
        send_far_halos(n, around[n] & jnp.logical_not(answered[n]))
    for n in range(4):
        @pl.when(around[n])
        def _():
            halo_out(n, near).start()
    for n in (2, 3, 0, 1):
        send_far_halos(n, jnp.logical_not(around[n]) if STEPS[n] > 0 else gx >= 0)

    @pl.when(half == 1)
    def _():
        for n in (0, 2):
            @pl.when(answers[n])
            def _():
                pl.semaphore_signal(ready.at[n], inc=1, device_id=nearest(-STEPS[n]), device_id_type=MESH)

    signal_blocks(join, lambda block: column > block)

    @pl.when(jnp.logical_not(near_first))
    def _():
        x_pass(near)
        pack_two(near)

    late_near = (half == 1) & (lax.rem(gx, 4) == 0) & (gx < 24)

    def send_near_halos(flag):
        for n in range(4):
            @pl.when(flag & (jnp.logical_not(wraps(STEPS[n])) | ((half == 1) & (STEPS[n] < 0))))
            def _():
                halo_out(n, near).start()

    send_near_halos(jnp.logical_not(late_near) | wraps(-2))

    def await_halos(numbers, side, block=None):
        for n in numbers:
            @pl.when(kept(side)[n])
            def _():
                halo_in(n, side, block).wait_recv()

    def relay_copy(slot, tile, count):
        return pltpu.make_async_remote_copy(
            src_ref=relay.at[tile, pl.ds(0, count)],
            dst_ref=relayed.at[slot, pl.ds(0, count)],
            send_sem=relay_send.at[tile],
            recv_sem=relay_recv.at[slot],
            device_id=(gx, tile),
            device_id_type=MESH,
        )

    def at_ends(act, *ends):
        for low in ends:
            for place, count in ((0, 3), (1, 1)):
                @pl.when(gx == (place if low else nx - 1 - place))
                def _():
                    act(low, count)

    def pass_on(side, low, count):
        ones, twos = (from_left, 2) if low else (from_right, 3)
        slot = 2 if side is near else 3

        def fill(block, core, target, place):
            here = lanes_of(block, core)
            value = tail_two[slot, :, here]
            if count == 3:
                target[place, 0] = value + ones[slot, 2, :, here]
                for pair in range(2):
                    target[place, 1 + pair] = ones[slot, pair, :, here]
            else:
                target[place, 0] = value

        wrapped_in(twos, side).wait_recv()
        if count == 3 and side is far:
            wrapped_in(twos - 2, side).wait_recv()
        elif count == 3:
            for block in range(blocks):
                wrapped_in(twos - 2, side, block).wait_recv()
        unpack_two(slot, [None, None, low, not low])

        @pl.loop(1 if side is near else 0, 2 * blocks)
        def _(j):
            block, core, tile = peer(side, j)
            fill(block, core, relay, tile)
            relay_copy(gy, tile, count).start()

        if side is near:
            fill(gy // 4, lax.rem(gy, 2), relayed, gy)

    await_halos((2, 3), far)
    unpack_two(far, kept(far))

    @pl.loop(0, blocks)
    def _(i):
        await_halos((0, 1), far, block_from_here(i))
        for j in range(2):
            block, core, tile = peer(far, 2 * i + j)
            combine(far, block, core, send, tile)

            @pl.when(half == 1)
            def _():
                tile_copy(tile).start()

    send_near_halos(late_near & jnp.logical_not(wraps(-2)))

    for n in (0, 2):
        @pl.when(answered[n])
        def _():
            pl.semaphore_wait(ready.at[n], 1)
        send_far_halos(n, answered[n])

    @pl.when(half == 0)
    def _():
        @pl.loop(0, blocks)
        def _(block):
            pl.semaphore_wait(go.at[block], 2)
            for core in range(2):
                tile_copy(block * 4 + far * 2 + core).start()

        at_ends(functools.partial(pass_on, far), False)

    await_halos(range(4), near)
    unpack_two(near, kept(near))
    @pl.when(column < blocks - 1)
    def _():
        pl.semaphore_wait(join, 2 * (blocks - 1 - column))

    @pl.loop(1, 2 * blocks)
    def _(j):
        block, core, tile = peer(near, j)
        combine(near, block, core, send, tile)
        tile_copy(tile).start()

    combine(near, gy // 4, lax.rem(gy, 2), got, gy)

    at_ends(functools.partial(pass_on, near), True, False)


    @pl.loop(1, 2 * blocks)
    def _(j):
        arrival(peer(near, j)[2]).wait_recv()

    @pl.loop(0, 2 * blocks)
    def _(j):
        arrival(peer(far, j)[2]).wait_recv()

    def take_over(low, count):
        def take(side, first, back):
            @pl.loop(first, 2 * blocks)
            def _(j):
                tile = peer(side, j)[2]
                relay_copy(tile, tile, count).wait_recv()

            @pl.loop(0, 2 * blocks)
            def _(j):
                tile, owner = peer(side, j)[2], peer(back, j)[2]
                if count == 3:
                    for pair in range(2):
                        value = relayed[tile, 1 + pair]
                        for n, rows in enumerate(spread_rows(value, 0.0) if low else spread_rows(0.0, value)):
                            got[owner, 2 * pair + n] += rows
                got[owner, 4] += relayed[tile, 0]

        take(near, 1, far)
        if not low:
            @pl.when(half == 1)
            def _():
                take(far, 0, near)

    at_ends(take_over, True, False)

    pairs = 2 * ny
    shape = (pairs, ROWS, TILE)
    wide = lax.broadcasted_iota(jnp.int32, (ny, ROWS, TILE), 2) % 2 == 0
    pairs_one = [swap(got[:, n], got[:, n + 1], wide, 1, 2) for n in (0, 2)]
    s, r = leading_lift(*(jnp.stack(both, axis=1).reshape(shape) for both in zip(*pairs_one)))
    slot = got[:, 4]
    under = pltpu.roll(slot, ROWS - 1, 1)

    def left(value):
        return pltpu.roll(value, TILE - 1, 2)

    even = jnp.stack([slot, under], axis=1).reshape(shape)
    odd = jnp.stack([left(slot), left(under)], axis=1).reshape(shape)
    coarse = leading_lift(even, odd)[0].reshape(ny, 2, ROWS, TILE)
    low, high = leading_lift(coarse[:, 0], coarse[:, 1])
    coarse = jnp.stack([low, high], axis=1).reshape(shape)
    corner = (lax.broadcasted_iota(jnp.int32, shape, 1) % 2 == 0) & (lax.broadcasted_iota(jnp.int32, shape, 2) % 2 == 0)
    out_ref[:, 0] = jnp.where(corner, coarse, s)
    out_ref[:, 1] = r

    for n in range(4):
        halo_out(n, near).wait_send()
    for n in (2, 3):
        halo_out(n, far).wait_send()

    @pl.loop(0, blocks)
    def _(i):
        for n in (0, 1):
            halo_out(n, far, block_from_here(i)).wait_send()

    @pl.loop(1, 2 * blocks)
    def _(j):
        tile_copy(peer(near, j)[2]).wait_send()

    @pl.loop(0, 2 * blocks)
    def _(j):
        tile_copy(peer(far, j)[2]).wait_send()

    def drain(low, count):
        @pl.loop(1, 2 * blocks)
        def _(j):
            relay_copy(gy, peer(near, j)[2], count).wait_send()

        if not low:
            @pl.when(half == 0)
            def _():
                @pl.loop(0, 2 * blocks)
                def _(j):
                    relay_copy(gy, peer(far, j)[2], count).wait_send()

    at_ends(drain, True, False)


def solution(mesh):
    nx, ny = mesh.shape["gx"], mesh.shape["gy"]
    length = ny * TILE
    half = length // 2

    def body(velocity):
        out = pl.pallas_call(
            functools.partial(kernel, nx, ny),
            out_shape=jax.ShapeDtypeStruct((2 * ny, 2, ROWS, TILE), F32),
            in_specs=[pl.BlockSpec(memory_space=pl.ANY)] * 2,
            out_specs=pl.BlockSpec(memory_space=pltpu.VMEM),
            scratch_shapes=[
                pltpu.VMEM((4, ROWS, length), F32),
                pltpu.VMEM((ROWS, TILE), F32),
                pltpu.VMEM((len(NAMES), ROWS, TILE), F32),
                pltpu.VMEM((4, ROWS, length), F32),
                pltpu.VMEM((2, ROWS, length), F32),
                pltpu.VMEM((2, 4, ROWS, half), F32),
                pltpu.VMEM((2, ROWS, half), F32),
                pltpu.VMEM((2, ROWS, half), F32),
                pltpu.VMEM((2, ROWS, half), F32),
                pltpu.VMEM((2, 3, ROWS, half), F32),
                pltpu.VMEM((2, 3, ROWS, half), F32),
                pltpu.VMEM((2, ROWS, 2 * TILE), F32),
                pltpu.VMEM((2, ROWS, 2 * TILE), F32),
                pltpu.VMEM((4, 3, ROWS, half), F32),
                pltpu.VMEM((4, 3, ROWS, half), F32),
                pltpu.VMEM((4, ROWS, 2 * TILE), F32),
                pltpu.VMEM((4, ROWS, 2 * TILE), F32),
                pltpu.VMEM((4, ROWS, half), F32),
                pltpu.VMEM((ny, 5, ROWS, TILE), F32),
                pltpu.VMEM((ny, 5, ROWS, TILE), F32),
                pltpu.VMEM((ny, 3, ROWS, TILE), F32),
                pltpu.VMEM((ny, 3, ROWS, TILE), F32),
                pltpu.SemaphoreType.DMA((2,)),
                pltpu.SemaphoreType.DMA((2, 4 + ny // 2)),
                pltpu.SemaphoreType.DMA((4, 4 + ny // 2)),
                pltpu.SemaphoreType.DMA((ny,)),
                pltpu.SemaphoreType.DMA((ny,)),
                pltpu.SemaphoreType.DMA((ny,)),
                pltpu.SemaphoreType.DMA((ny,)),
                pltpu.SemaphoreType.REGULAR((ny // 4,)),
                pltpu.SemaphoreType.REGULAR((4,)),
                pltpu.SemaphoreType.REGULAR,
            ],
            compiler_params=pltpu.CompilerParams(collective_id=0, has_side_effects=True, vmem_limit_bytes=24576 * 1024),
        )(pltpu.with_memory_space_constraint(velocity, pltpu.HBM), pltpu.with_memory_space_constraint(jnp.asarray(COLUMNS), pltpu.HBM))
        return out.reshape(4 * ny, ROWS, TILE)

    return jax.shard_map(
        body, mesh=mesh, in_specs=(P("gy", "gx", None),), out_specs=P(None, "gx", "gy"), check_vma=False
    )
```

```python
import functools

import jax
import jax.numpy as jnp
import numpy as np
from jax import lax
from jax.experimental import pallas as pl
from jax.experimental.pallas import tpu as pltpu
from jax.sharding import PartitionSpec as P

PREDICT_FIRST = -1.586134342
UPDATE_FIRST = -0.05298011854
PREDICT_SECOND = 0.8829110762
UPDATE_SECOND = 0.4435068522
SCALE_LOW = 1.149604398
SCALE_HIGH = 1.0 / 1.149604398

MESH = pl.DeviceIdType.MESH
ROWS = 8
STEPS = (1, -1, 2, -2)
TILE = 128
F32 = jnp.float32


def lift_matrix(extent):
    table = np.eye(extent)
    s, r = table[0::2], table[1::2]
    r = r + PREDICT_FIRST * (s + np.roll(s, -1, 0))
    s = s + UPDATE_FIRST * (r + np.roll(r, 1, 0))
    r = r + PREDICT_SECOND * (s + np.roll(s, -1, 0))
    s = s + UPDATE_SECOND * (r + np.roll(r, 1, 0))
    out = np.empty((extent, extent))
    out[0::2], out[1::2] = s * SCALE_LOW, r * SCALE_HIGH
    return out


LOW_TAPS = [float(tap) for tap in lift_matrix(32)[16, 16:21]]
HIGH_TAPS = [float(tap) for tap in lift_matrix(32)[17, 17:21]]


def row_operators():
    extent, mine = 128, 64
    first = lift_matrix(extent)
    second = lift_matrix(extent // 2) @ first[0::2]
    wide = np.zeros((extent, extent))
    wide[0::2] = second

    def block(table, step):
        start = mine + ROWS * step
        return table[start : start + ROWS, mine : mine + ROWS]

    return {step: block(first, step) for step in (-1, 0, 1)}, {step: block(wide, step) for step in (-2, -1, 0, 1, 2)}


def coefficient_columns():
    first, second = row_operators()
    columns, names = [], {}

    def add(name, column):
        if np.any(column != 0):
            names[name] = len(columns)
            columns.append(column)

    halo = first[1] + first[-1]
    assert not np.any((first[1] != 0) & (first[-1] != 0).any(axis=1, keepdims=True))
    even = np.arange(ROWS) // 2 * 2
    for j in range(ROWS):
        add(("own", j), first[0][:, j])
        add(("halo", j), halo[:, j])
        for step in (-1, 0, 1, 2):
            add((step, j), second[step][even, j])
    tail = np.zeros(ROWS)
    tail[4:] = second[-2][[4, 4, 6, 6], 0]
    add(("tail", 0), tail)
    table = np.zeros((ROWS, TILE), np.float32)
    table[:, : len(columns)] = np.stack(columns, 1)
    return table, names


COLUMNS, NAMES = coefficient_columns()


def lane_lift(s, r, stride):
    axis, length = s.ndim - 1, s.shape[-1]

    def at(a, pairs):
        return pltpu.roll(a, (-pairs * stride) % length, axis) if pairs else a

    low, high = LOW_TAPS, HIGH_TAPS
    s_next, s_last, r_next, r_last = at(s, 1), at(s, -1), at(r, 1), at(r, -1)
    s_after, s_before, r_before = at(s, 2), at(s, -2), at(r, -2)
    s_out = (low[0] * s + low[2] * (s_next + s_last)) + low[4] * (s_after + s_before)
    s_out = s_out + (low[1] * (r + r_last) + low[3] * (r_next + r_before))
    r_out = (high[0] * r + high[2] * (r_next + r_last)) + (high[1] * (s + s_next) + high[3] * (s_last + s_after))
    return s_out, r_out


def swap(a, b, low, stride, axis):
    size = a.shape[axis]
    return jnp.where(low, a, pltpu.roll(b, stride, axis)), jnp.where(low, pltpu.roll(a, size - stride, axis), b)


def leading_lift(s, r):
    def after(a):
        return jnp.concatenate([a[1:], a[:1]], axis=0)

    def before(a):
        return jnp.concatenate([a[-1:], a[:-1]], axis=0)

    r = r + PREDICT_FIRST * (s + after(s))
    s = s + UPDATE_FIRST * (r + before(r))
    r = r + PREDICT_SECOND * (s + after(s))
    s = s + UPDATE_SECOND * (r + before(r))
    return s * SCALE_LOW, r * SCALE_HIGH


def kernel(nx, ny, v_hbm, table_hbm, out_ref, v_ref, table_ref, weights, y_one, y_two, own, own_two, far_two, near_two, go_right,
           go_left, go_right_two, go_left_two, from_left, from_right, from_left_two, from_right_two, tail_two, send, got,
           relay, relayed, in_sem, halo_send, halo_recv, send_sem, recv_sem, relay_send, relay_recv, go, ready, join):
    gx, gy = lax.axis_index("gx"), lax.axis_index("gy")
    half = (gy // 2) % 2
    blocks = ny // 4

    load = pltpu.make_async_copy(v_hbm, v_ref, in_sem.at[0])
    load.start()
    load_table = pltpu.make_async_copy(table_hbm, table_ref, in_sem.at[1])
    load_table.start()

    other = gy + 2 - 4 * half

    def wraps(step):
        return jnp.logical_or(gx + step < 0, gx + step >= nx)

    def beside(step):
        return (lax.rem(gx + step + nx, nx), gy)

    def nearest(step):
        return (lax.rem(gx + step + nx, nx), jnp.where(wraps(step), other, gy))

    def peer(side, j):
        block = lax.rem(gy // 4 + j // 2, blocks)
        core = lax.rem(gy + j, 2)
        return block, core, block * 4 + side * 2 + core

    barrier = pltpu.get_barrier_semaphore()
    far, near = 1 - half, half
    answered = [wraps(step) & (half == 0) if step > 0 else gx < 0 for step in STEPS]
    answers = [wraps(-step) & (half == 1) if step > 0 else gx < 0 for step in STEPS]
    for n in range(4):
        back = (1, 0, 3, 2)[n]

        @pl.when(jnp.logical_not(answers[back]))
        def _():
            pl.semaphore_signal(barrier, inc=1, device_id=nearest(STEPS[n]), device_id_type=MESH)
    column = gy // 4
    pl.semaphore_signal(barrier, inc=1, device_id=(gx, peer(near, 1)[2]), device_id_type=MESH)

    def signal_blocks(semaphore, flag):
        for block in range(blocks):
            @pl.when(flag(block))
            def _():
                for core in range(2):
                    tile = block * 4 + near * 2 + core
                    pl.semaphore_signal(semaphore, inc=1, device_id=(gx, tile), device_id_type=MESH)

    signal_blocks(barrier, lambda block: column < block)

    def greet_far(semaphore):
        for j in range(2 * blocks):
            pl.semaphore_signal(semaphore, inc=1, device_id=(gx, peer(far, j)[2]), device_id_type=MESH)

    heard = (half == 0)
    for n in range(4):
        @pl.when(wraps(-STEPS[n]) & (heard if STEPS[n] < 0 else gx >= 0))
        def _():
            pl.semaphore_signal(barrier, inc=1, device_id=beside(-STEPS[n]), device_id_type=MESH)

    @pl.when(half == 0)
    def _():
        greet_far(barrier)

    load_table.wait()
    for at in range(len(NAMES)):
        weights[at] = jnp.broadcast_to(table_ref[:, at : at + 1], (ROWS, TILE))
    load.wait()

    lane = lax.broadcasted_iota(jnp.int32, (ROWS, TILE), 1)
    row = lax.broadcasted_iota(jnp.int32, (ROWS, TILE), 0)
    low_row = row < 4
    even_row = row % 2 == 0

    def low_lanes(stride):
        return jnp.concatenate([(lane // stride) % 2] * ny, axis=1) == 0

    lows = []
    for pair in range(2):
        s, r = swap(v_ref[2 * pair], v_ref[2 * pair + 1], low_lanes(1), 1, 1)
        s, r = lane_lift(s, r, 2)
        y_one[2 * pair] = s
        y_one[2 * pair + 1] = r
        lows.append(s)
    s, r = lane_lift(*swap(*lows, low_lanes(2), 2, 1), 4)
    y_two[0], y_two[1] = swap(s, r, low_lanes(2), 2, 1)

    def weigh(total, name, value):
        if name not in NAMES:
            return total
        term = weights[NAMES[name]] * value
        return term if total is None else total + term

    def down(value, k):
        return value if k % ROWS == 0 or isinstance(value, float) else pltpu.roll(value, k % ROWS, 0)

    def x_pass(side):
        @pl.loop(0, 2 * blocks)
        def _(p):
            tile = (p // 2) * 4 + side * 2 + p % 2
            lanes = pl.ds(pl.multiple_of(tile * TILE, TILE), TILE)
            here = pl.ds(pl.multiple_of(p * TILE, TILE), TILE)

            def spread(ref, z, j):
                return jnp.broadcast_to(ref[z, j : j + 1, lanes], (ROWS, TILE))

            mine, halos = [None] * 4, [None] * 4
            for j in range(ROWS):
                for z in range(4):
                    value = spread(y_one, z, j)
                    mine[z] = weigh(mine[z], ("own", j), value)
                    halos[z] = weigh(halos[z], ("halo", j), value)
            for z in range(4):
                own[side, z, :, here] = mine[z]
            for pair in range(2):
                a, b = halos[2 * pair], halos[2 * pair + 1]
                go_right[side, pair, :, here] = jnp.where(low_row, a, down(b, 4))
                go_left[side, pair, :, here] = jnp.where(low_row, down(a, 4), b)
            sums = {step: None for step in (-1, 0, 1, 2)}
            for j in range(ROWS):
                value = jnp.where(even_row, spread(y_two, 0, j), spread(y_two, 1, j))
                if j == 0:
                    near_two[side, :, here] = value
                for step in sums:
                    sums[step] = weigh(sums[step], (step, j), value)
            own_two[side, :, here] = sums[0]
            go_right[side, 2, :, here] = sums[1]
            go_left[side, 2, :, here] = sums[-1]
            far_two[side, :, here] = sums[2]

    wide_row = lax.broadcasted_iota(jnp.int32, (ROWS, 2 * TILE), 0)

    def pack_two(side):
        for source, target in ((far_two, go_right_two), (near_two, go_left_two)):
            packed = source[side, :, 0 : 2 * TILE]
            for block in range(1, blocks):
                value = down(source[side, :, block * 2 * TILE : (block + 1) * 2 * TILE], 2 * block)
                packed = jnp.where(wide_row // 2 == block, value, packed)
            target[side] = packed

    messages = (
        (go_right, from_left),
        (go_left, from_right),
        (go_right_two, from_left_two),
        (go_left_two, from_right_two),
    )

    def halo_copy(n, side, slot, device, block=None):
        source, target = messages[n][0].at[side], messages[n][1].at[slot]
        at = n
        if block is not None:
            lanes = pl.ds(pl.multiple_of(block * 2 * TILE, 2 * TILE), 2 * TILE)
            source, target = source.at[:, :, lanes], target.at[:, :, lanes]
            at = 4 + n * blocks + block
        return pltpu.make_async_remote_copy(
            src_ref=source,
            dst_ref=target,
            send_sem=halo_send.at[side, at],
            recv_sem=halo_recv.at[slot, at],
            device_id=device,
            device_id_type=MESH,
        )

    def halo_out(n, side, block=None):
        step = STEPS[n]
        if side is near:
            by_other = wraps(step) & (half == 1) & (step < 0)
            gx_to, gy_to = beside(step)
            return halo_copy(n, side, jnp.where(by_other, 3, side), (gx_to, jnp.where(by_other, other, gy_to)), block)
        return halo_copy(n, side, jnp.where(wraps(step), 2, side), nearest(step), block)

    def halo_in(n, side, block=None):
        return halo_copy(n, side, side, beside(STEPS[n]), block)

    def wrapped_in(n, side, block=None):
        return halo_copy(n, side, 2 if side is near else 3, beside(STEPS[n]), block)

    def block_from_here(i):
        column, back = gy // 4, blocks - 1 - i
        return lax.rem(column // 2 + back // 2, 2) * 2 + lax.rem(column + back, 2)

    came = [wraps(-step) for step in STEPS]
    straight = [jnp.logical_not(flag) for flag in came]

    def kept(side):
        return straight if side is far else [True, straight[1] | (half == 0), True, straight[3] | (half == 0)]

    def only(flag, value):
        if isinstance(flag, bool):
            return value if flag else 0.0
        return jnp.where(flag, value, 0.0)

    def unpack_two(slot, keep):
        tail = NAMES[("tail", 0)]
        tails = jnp.broadcast_to(table_ref[:, tail : tail + 1], (ROWS, 2 * TILE))
        for block in range(blocks):
            head = jnp.where(wide_row < 2, down(from_left_two[slot], ROWS - 2 * block), 0.0)
            late = from_right_two[slot]
            late = jnp.where(wide_row < 6, down(late, 4 - 2 * block), down(late, 6 - 2 * block))
            tail_two[slot, :, block * 2 * TILE : (block + 1) * 2 * TILE] = only(keep[2], head) + only(keep[3], tails * late)

    def spread_rows(a, b):
        return [jnp.where(low_row, a, down(b, 4)), jnp.where(low_row, down(a, 4), b)]

    def halo_tiles(slot, keep, here):
        tiles = []
        for pair in range(2):
            tiles += spread_rows(only(keep[0], from_left[slot, pair, :, here]), only(keep[1], from_right[slot, pair, :, here]))
        a, b = only(keep[0], from_left[slot, 2, :, here]), only(keep[1], from_right[slot, 2, :, here])
        return tiles + [tail_two[slot, :, here] + (a + b)]

    def lanes_of(block, core):
        return pl.ds(pl.multiple_of((block * 2 + core) * TILE, TILE), TILE)

    def combine(side, block, core, target, slot):
        here = lanes_of(block, core)
        tiles = halo_tiles(side, kept(side), here)
        for n in range(4):
            target[slot, n] = own[side, n, :, here] + tiles[n]
        target[slot, 4] = own_two[side, :, here] + tiles[4]

    def tile_copy(tile):
        return pltpu.make_async_remote_copy(
            src_ref=send.at[tile],
            dst_ref=got.at[gy],
            send_sem=send_sem.at[tile],
            recv_sem=recv_sem.at[gy],
            device_id=(gx, tile),
            device_id_type=MESH,
        )

    def arrival(tile):
        return pltpu.make_async_remote_copy(
            src_ref=send.at[tile],
            dst_ref=got.at[tile],
            send_sem=send_sem.at[tile],
            recv_sem=recv_sem.at[tile],
            device_id=(gx, tile),
            device_id_type=MESH,
        )

    x_pass(far)
    pack_two(far)
    late_greetings = jnp.where(wraps(1), 2, jnp.where(wraps(2), 1, 0)) * half
    late_greetings += jnp.where(wraps(-1), 2, jnp.where(wraps(-2), 1, 0)) * jnp.where(heard, 1, 0)
    near_first = (half == 0) | wraps(8)

    @pl.when(near_first)
    def _():
        x_pass(near)
        pack_two(near)

    pl.semaphore_wait(barrier, 5 + 2 * column + 2 * blocks * half + late_greetings)

    @pl.when(half == 1)
    def _():
        greet_far(go.at[column])

    def send_far_halos(n, condition):
        @pl.when(condition)
        def _():
            if n > 1:
                halo_out(n, far).start()
            else:
                @pl.loop(0, blocks)
                def _(i):
                    halo_out(n, far, block_from_here(i)).start()

    around = [wraps(step) & (heard if step < 0 else gx >= 0) for step in STEPS]
    for n in (2, 0):
        send_far_halos(n, around[n] & jnp.logical_not(answered[n]))
    for n in range(4):
        @pl.when(around[n])
        def _():
            halo_out(n, near).start()
    for n in (2, 3, 0, 1):
        send_far_halos(n, jnp.logical_not(around[n]) if STEPS[n] > 0 else gx >= 0)

    @pl.when(half == 1)
    def _():
        for n in (0, 2):
            @pl.when(answers[n])
            def _():
                pl.semaphore_signal(ready.at[n], inc=1, device_id=nearest(-STEPS[n]), device_id_type=MESH)

    signal_blocks(join, lambda block: column > block)

    @pl.when(jnp.logical_not(near_first))
    def _():
        x_pass(near)
        pack_two(near)

    late_near = (half == 1) & (lax.rem(gx, 4) == 0) & (gx < 24)

    def send_near_halos(flag):
        for n in range(4):
            @pl.when(flag & (jnp.logical_not(wraps(STEPS[n])) | ((half == 1) & (STEPS[n] < 0))))
            def _():
                halo_out(n, near).start()

    send_near_halos(jnp.logical_not(late_near) | wraps(-2))

    def await_halos(numbers, side, block=None):
        for n in numbers:
            @pl.when(kept(side)[n])
            def _():
                halo_in(n, side, block).wait_recv()

    def relay_copy(slot, tile, count):
        return pltpu.make_async_remote_copy(
            src_ref=relay.at[tile, pl.ds(0, count)],
            dst_ref=relayed.at[slot, pl.ds(0, count)],
            send_sem=relay_send.at[tile],
            recv_sem=relay_recv.at[slot],
            device_id=(gx, tile),
            device_id_type=MESH,
        )

    def at_ends(act, *ends):
        for low in ends:
            for place, count in ((0, 3), (1, 1)):
                @pl.when(gx == (place if low else nx - 1 - place))
                def _():
                    act(low, count)

    def pass_on(side, low, count):
        ones, twos = (from_left, 2) if low else (from_right, 3)
        slot = 2 if side is near else 3

        def fill(block, core, target, place):
            here = lanes_of(block, core)
            value = tail_two[slot, :, here]
            if count == 3:
                target[place, 0] = value + ones[slot, 2, :, here]
                for pair in range(2):
                    target[place, 1 + pair] = ones[slot, pair, :, here]
            else:
                target[place, 0] = value

        wrapped_in(twos, side).wait_recv()
        if count == 3 and side is far:
            wrapped_in(twos - 2, side).wait_recv()
        elif count == 3:
            for block in range(blocks):
                wrapped_in(twos - 2, side, block).wait_recv()
        unpack_two(slot, [None, None, low, not low])

        @pl.loop(1 if side is near else 0, 2 * blocks)
        def _(j):
            block, core, tile = peer(side, j)
            fill(block, core, relay, tile)
            relay_copy(gy, tile, count).start()

        if side is near:
            fill(gy // 4, lax.rem(gy, 2), relayed, gy)

    await_halos((2, 3), far)
    unpack_two(far, kept(far))

    @pl.loop(0, blocks)
    def _(i):
        await_halos((0, 1), far, block_from_here(i))
        for j in range(2):
            block, core = block_from_here(i), lax.rem(gy + j, 2)
            tile = block * 4 + far * 2 + core
            combine(far, block, core, send, tile)

            @pl.when(half == 1)
            def _():
                tile_copy(tile).start()

    send_near_halos(late_near & jnp.logical_not(wraps(-2)))

    for n in (0, 2):
        @pl.when(answered[n])
        def _():
            pl.semaphore_wait(ready.at[n], 1)
        send_far_halos(n, answered[n])

    @pl.when(half == 0)
    def _():
        @pl.loop(0, blocks)
        def _(block):
            pl.semaphore_wait(go.at[block], 2)
            for core in range(2):
                tile_copy(block * 4 + far * 2 + core).start()

        at_ends(functools.partial(pass_on, far), False)

    await_halos(range(4), near)
    unpack_two(near, kept(near))
    @pl.when(column < blocks - 1)
    def _():
        pl.semaphore_wait(join, 2 * (blocks - 1 - column))

    @pl.loop(1, 2 * blocks)
    def _(j):
        block, core, tile = peer(near, j)
        combine(near, block, core, send, tile)
        tile_copy(tile).start()

    combine(near, gy // 4, lax.rem(gy, 2), got, gy)

    at_ends(functools.partial(pass_on, near), True, False)


    @pl.loop(1, 2 * blocks)
    def _(j):
        arrival(peer(near, j)[2]).wait_recv()

    @pl.loop(0, 2 * blocks)
    def _(j):
        arrival(peer(far, j)[2]).wait_recv()

    def take_over(low, count):
        def take(side, first, back):
            @pl.loop(first, 2 * blocks)
            def _(j):
                tile = peer(side, j)[2]
                relay_copy(tile, tile, count).wait_recv()

            @pl.loop(0, 2 * blocks)
            def _(j):
                tile, owner = peer(side, j)[2], peer(back, j)[2]
                if count == 3:
                    for pair in range(2):
                        value = relayed[tile, 1 + pair]
                        for n, rows in enumerate(spread_rows(value, 0.0) if low else spread_rows(0.0, value)):
                            got[owner, 2 * pair + n] += rows
                got[owner, 4] += relayed[tile, 0]

        take(near, 1, far)
        if not low:
            @pl.when(half == 1)
            def _():
                take(far, 0, near)

    at_ends(take_over, True, False)

    pairs = 2 * ny
    shape = (pairs, ROWS, TILE)
    wide = lax.broadcasted_iota(jnp.int32, (ny, ROWS, TILE), 2) % 2 == 0
    pairs_one = [swap(got[:, n], got[:, n + 1], wide, 1, 2) for n in (0, 2)]
    s, r = leading_lift(*(jnp.stack(both, axis=1).reshape(shape) for both in zip(*pairs_one)))
    slot = got[:, 4]
    under = pltpu.roll(slot, ROWS - 1, 1)

    def left(value):
        return pltpu.roll(value, TILE - 1, 2)

    even = jnp.stack([slot, under], axis=1).reshape(shape)
    odd = jnp.stack([left(slot), left(under)], axis=1).reshape(shape)
    coarse = leading_lift(even, odd)[0].reshape(ny, 2, ROWS, TILE)
    low, high = leading_lift(coarse[:, 0], coarse[:, 1])
    coarse = jnp.stack([low, high], axis=1).reshape(shape)
    corner = (lax.broadcasted_iota(jnp.int32, shape, 1) % 2 == 0) & (lax.broadcasted_iota(jnp.int32, shape, 2) % 2 == 0)
    out_ref[:, 0] = jnp.where(corner, coarse, s)
    out_ref[:, 1] = r

    for n in range(4):
        halo_out(n, near).wait_send()
    for n in (2, 3):
        halo_out(n, far).wait_send()

    @pl.loop(0, blocks)
    def _(i):
        for n in (0, 1):
            halo_out(n, far, block_from_here(i)).wait_send()

    @pl.loop(1, 2 * blocks)
    def _(j):
        tile_copy(peer(near, j)[2]).wait_send()

    @pl.loop(0, 2 * blocks)
    def _(j):
        tile_copy(peer(far, j)[2]).wait_send()

    def drain(low, count):
        @pl.loop(1, 2 * blocks)
        def _(j):
            relay_copy(gy, peer(near, j)[2], count).wait_send()

        if not low:
            @pl.when(half == 0)
            def _():
                @pl.loop(0, 2 * blocks)
                def _(j):
                    relay_copy(gy, peer(far, j)[2], count).wait_send()

    at_ends(drain, True, False)


def solution(mesh):
    nx, ny = mesh.shape["gx"], mesh.shape["gy"]
    length = ny * TILE
    half = length // 2

    def body(velocity):
        out = pl.pallas_call(
            functools.partial(kernel, nx, ny),
            out_shape=jax.ShapeDtypeStruct((2 * ny, 2, ROWS, TILE), F32),
            in_specs=[pl.BlockSpec(memory_space=pl.ANY)] * 2,
            out_specs=pl.BlockSpec(memory_space=pltpu.VMEM),
            scratch_shapes=[
                pltpu.VMEM((4, ROWS, length), F32),
                pltpu.VMEM((ROWS, TILE), F32),
                pltpu.VMEM((len(NAMES), ROWS, TILE), F32),
                pltpu.VMEM((4, ROWS, length), F32),
                pltpu.VMEM((2, ROWS, length), F32),
                pltpu.VMEM((2, 4, ROWS, half), F32),
                pltpu.VMEM((2, ROWS, half), F32),
                pltpu.VMEM((2, ROWS, half), F32),
                pltpu.VMEM((2, ROWS, half), F32),
                pltpu.VMEM((2, 3, ROWS, half), F32),
                pltpu.VMEM((2, 3, ROWS, half), F32),
                pltpu.VMEM((2, ROWS, 2 * TILE), F32),
                pltpu.VMEM((2, ROWS, 2 * TILE), F32),
                pltpu.VMEM((4, 3, ROWS, half), F32),
                pltpu.VMEM((4, 3, ROWS, half), F32),
                pltpu.VMEM((4, ROWS, 2 * TILE), F32),
                pltpu.VMEM((4, ROWS, 2 * TILE), F32),
                pltpu.VMEM((4, ROWS, half), F32),
                pltpu.VMEM((ny, 5, ROWS, TILE), F32),
                pltpu.VMEM((ny, 5, ROWS, TILE), F32),
                pltpu.VMEM((ny, 3, ROWS, TILE), F32),
                pltpu.VMEM((ny, 3, ROWS, TILE), F32),
                pltpu.SemaphoreType.DMA((2,)),
                pltpu.SemaphoreType.DMA((2, 4 + ny // 2)),
                pltpu.SemaphoreType.DMA((4, 4 + ny // 2)),
                pltpu.SemaphoreType.DMA((ny,)),
                pltpu.SemaphoreType.DMA((ny,)),
                pltpu.SemaphoreType.DMA((ny,)),
                pltpu.SemaphoreType.DMA((ny,)),
                pltpu.SemaphoreType.REGULAR((ny // 4,)),
                pltpu.SemaphoreType.REGULAR((4,)),
                pltpu.SemaphoreType.REGULAR,
            ],
            compiler_params=pltpu.CompilerParams(collective_id=0, has_side_effects=True, vmem_limit_bytes=24576 * 1024),
        )(pltpu.with_memory_space_constraint(velocity, pltpu.HBM), pltpu.with_memory_space_constraint(jnp.asarray(COLUMNS), pltpu.HBM))
        return out.reshape(4 * ny, ROWS, TILE)

    return jax.shard_map(
        body, mesh=mesh, in_specs=(P("gy", "gx", None),), out_specs=P(None, "gx", "gy"), check_vma=False
    )
```

```python
import functools

import jax
import jax.numpy as jnp
import numpy as np
from jax import lax
from jax.experimental import pallas as pl
from jax.experimental.pallas import tpu as pltpu
from jax.sharding import PartitionSpec as P

PREDICT_FIRST = -1.586134342
UPDATE_FIRST = -0.05298011854
PREDICT_SECOND = 0.8829110762
UPDATE_SECOND = 0.4435068522
SCALE_LOW = 1.149604398
SCALE_HIGH = 1.0 / 1.149604398

MESH = pl.DeviceIdType.MESH
ROWS = 8
STEPS = (1, -1, 2, -2)
TILE = 128
F32 = jnp.float32


def lift_matrix(extent):
    table = np.eye(extent)
    s, r = table[0::2], table[1::2]
    r = r + PREDICT_FIRST * (s + np.roll(s, -1, 0))
    s = s + UPDATE_FIRST * (r + np.roll(r, 1, 0))
    r = r + PREDICT_SECOND * (s + np.roll(s, -1, 0))
    s = s + UPDATE_SECOND * (r + np.roll(r, 1, 0))
    out = np.empty((extent, extent))
    out[0::2], out[1::2] = s * SCALE_LOW, r * SCALE_HIGH
    return out


LOW_TAPS = [float(tap) for tap in lift_matrix(32)[16, 16:21]]
HIGH_TAPS = [float(tap) for tap in lift_matrix(32)[17, 17:21]]


def row_operators():
    extent, mine = 128, 64
    first = lift_matrix(extent)
    second = lift_matrix(extent // 2) @ first[0::2]
    wide = np.zeros((extent, extent))
    wide[0::2] = second

    def block(table, step):
        start = mine + ROWS * step
        return table[start : start + ROWS, mine : mine + ROWS]

    return {step: block(first, step) for step in (-1, 0, 1)}, {step: block(wide, step) for step in (-2, -1, 0, 1, 2)}


def coefficient_columns():
    first, second = row_operators()
    columns, names = [], {}

    def add(name, column):
        if np.any(column != 0):
            names[name] = len(columns)
            columns.append(column)

    halo = first[1] + first[-1]
    assert not np.any((first[1] != 0) & (first[-1] != 0).any(axis=1, keepdims=True))
    even = np.arange(ROWS) // 2 * 2
    for j in range(ROWS):
        add(("own", j), first[0][:, j])
        add(("halo", j), halo[:, j])
        for step in (-1, 0, 1, 2):
            add((step, j), second[step][even, j])
    tail = np.zeros(ROWS)
    tail[4:] = second[-2][[4, 4, 6, 6], 0]
    add(("tail", 0), tail)
    table = np.zeros((ROWS, TILE), np.float32)
    table[:, : len(columns)] = np.stack(columns, 1)
    return table, names


COLUMNS, NAMES = coefficient_columns()


def lane_lift(s, r, stride):
    axis, length = s.ndim - 1, s.shape[-1]

    def at(a, pairs):
        return pltpu.roll(a, (-pairs * stride) % length, axis) if pairs else a

    low, high = LOW_TAPS, HIGH_TAPS
    s_next, s_last, r_next, r_last = at(s, 1), at(s, -1), at(r, 1), at(r, -1)
    s_after, s_before, r_before = at(s, 2), at(s, -2), at(r, -2)
    s_out = (low[0] * s + low[2] * (s_next + s_last)) + low[4] * (s_after + s_before)
    s_out = s_out + (low[1] * (r + r_last) + low[3] * (r_next + r_before))
    r_out = (high[0] * r + high[2] * (r_next + r_last)) + (high[1] * (s + s_next) + high[3] * (s_last + s_after))
    return s_out, r_out


def swap(a, b, low, stride, axis):
    size = a.shape[axis]
    return jnp.where(low, a, pltpu.roll(b, stride, axis)), jnp.where(low, pltpu.roll(a, size - stride, axis), b)


def leading_lift(s, r):
    def after(a):
        return jnp.concatenate([a[1:], a[:1]], axis=0)

    def before(a):
        return jnp.concatenate([a[-1:], a[:-1]], axis=0)

    r = r + PREDICT_FIRST * (s + after(s))
    s = s + UPDATE_FIRST * (r + before(r))
    r = r + PREDICT_SECOND * (s + after(s))
    s = s + UPDATE_SECOND * (r + before(r))
    return s * SCALE_LOW, r * SCALE_HIGH


def kernel(nx, ny, v_hbm, table_hbm, got, v_ref, table_ref, weights, y_one, y_two, own, own_two, far_two, near_two, go_right,
           go_left, go_right_two, go_left_two, from_left, from_right, from_left_two, from_right_two, tail_two, send,
           relay, relayed, in_sem, halo_send, halo_recv, send_sem, recv_sem, relay_send, relay_recv, go, ready, join):
    gx, gy = lax.axis_index("gx"), lax.axis_index("gy")
    half = (gy // 2) % 2
    blocks = ny // 4

    loads = [pltpu.make_async_copy(v_hbm.at[pl.ds(2 * pair, 2)], v_ref.at[pl.ds(2 * pair, 2)], in_sem.at[pair]) for pair in range(2)]
    load_table = pltpu.make_async_copy(table_hbm, table_ref, in_sem.at[2])
    loads[0].start()
    load_table.start()
    loads[1].start()

    other = gy + 2 - 4 * half

    def wraps(step):
        return jnp.logical_or(gx + step < 0, gx + step >= nx)

    def beside(step):
        return (lax.rem(gx + step + nx, nx), gy)

    def nearest(step):
        return (lax.rem(gx + step + nx, nx), jnp.where(wraps(step), other, gy))

    def peer(side, j):
        block = lax.rem(gy // 4 + j // 2, blocks)
        core = lax.rem(gy + j, 2)
        return block, core, block * 4 + side * 2 + core

    barrier = pltpu.get_barrier_semaphore()
    far, near = 1 - half, half
    answered = [wraps(step) & (half == 0) if step > 0 else gx < 0 for step in STEPS]
    answers = [wraps(-step) & (half == 1) if step > 0 else gx < 0 for step in STEPS]
    for n in range(4):
        back = (1, 0, 3, 2)[n]

        @pl.when(jnp.logical_not(answers[back]))
        def _():
            pl.semaphore_signal(barrier, inc=1, device_id=nearest(STEPS[n]), device_id_type=MESH)
    column = gy // 4
    pl.semaphore_signal(barrier, inc=1, device_id=(gx, peer(near, 1)[2]), device_id_type=MESH)

    def signal_blocks(semaphore, flag):
        for block in range(blocks):
            @pl.when(flag(block))
            def _():
                for core in range(2):
                    tile = block * 4 + near * 2 + core
                    pl.semaphore_signal(semaphore, inc=1, device_id=(gx, tile), device_id_type=MESH)

    signal_blocks(barrier, lambda block: column < block)

    def greet_far(semaphore):
        for j in range(2 * blocks):
            pl.semaphore_signal(semaphore, inc=1, device_id=(gx, peer(far, j)[2]), device_id_type=MESH)

    heard = (half == 0)
    for n in range(4):
        @pl.when(wraps(-STEPS[n]) & (heard if STEPS[n] < 0 else gx >= 0))
        def _():
            pl.semaphore_signal(barrier, inc=1, device_id=beside(-STEPS[n]), device_id_type=MESH)

    @pl.when(half == 0)
    def _():
        greet_far(barrier)

    load_table.wait()
    for at in range(len(NAMES)):
        weights[at] = jnp.broadcast_to(table_ref[:, at : at + 1], (ROWS, TILE))

    lane = lax.broadcasted_iota(jnp.int32, (ROWS, TILE), 1)
    row = lax.broadcasted_iota(jnp.int32, (ROWS, TILE), 0)
    low_row = row < 4
    even_row = row % 2 == 0

    def low_lanes(stride):
        return jnp.concatenate([(lane // stride) % 2] * ny, axis=1) == 0

    lows = []
    for pair in range(2):
        loads[pair].wait()
        s, r = swap(v_ref[2 * pair], v_ref[2 * pair + 1], low_lanes(1), 1, 1)
        s, r = lane_lift(s, r, 2)
        y_one[2 * pair] = s
        y_one[2 * pair + 1] = r
        lows.append(s)
    s, r = lane_lift(*swap(*lows, low_lanes(2), 2, 1), 4)
    y_two[0], y_two[1] = swap(s, r, low_lanes(2), 2, 1)

    def weigh(total, name, value):
        if name not in NAMES:
            return total
        term = weights[NAMES[name]] * value
        return term if total is None else total + term

    def down(value, k):
        return value if k % ROWS == 0 or isinstance(value, float) else pltpu.roll(value, k % ROWS, 0)

    def x_pass(side):
        @pl.loop(0, 2 * blocks)
        def _(p):
            tile = (p // 2) * 4 + side * 2 + p % 2
            lanes = pl.ds(pl.multiple_of(tile * TILE, TILE), TILE)
            here = pl.ds(pl.multiple_of(p * TILE, TILE), TILE)

            def spread(ref, z, j):
                return jnp.broadcast_to(ref[z, j : j + 1, lanes], (ROWS, TILE))

            mine, halos = [None] * 4, [None] * 4
            for j in range(ROWS):
                for z in range(4):
                    value = spread(y_one, z, j)
                    mine[z] = weigh(mine[z], ("own", j), value)
                    halos[z] = weigh(halos[z], ("halo", j), value)
            for z in range(4):
                own[side, z, :, here] = mine[z]
            for pair in range(2):
                a, b = halos[2 * pair], halos[2 * pair + 1]
                go_right[side, pair, :, here] = jnp.where(low_row, a, down(b, 4))
                go_left[side, pair, :, here] = jnp.where(low_row, down(a, 4), b)
            sums = {step: None for step in (-1, 0, 1, 2)}
            for j in range(ROWS):
                value = jnp.where(even_row, spread(y_two, 0, j), spread(y_two, 1, j))
                if j == 0:
                    near_two[side, :, here] = value
                for step in sums:
                    sums[step] = weigh(sums[step], (step, j), value)
            own_two[side, :, here] = sums[0]
            go_right[side, 2, :, here] = sums[1]
            go_left[side, 2, :, here] = sums[-1]
            far_two[side, :, here] = sums[2]

    wide_row = lax.broadcasted_iota(jnp.int32, (ROWS, 2 * TILE), 0)

    def pack_two(side):
        for source, target in ((far_two, go_right_two), (near_two, go_left_two)):
            packed = source[side, :, 0 : 2 * TILE]
            for block in range(1, blocks):
                value = down(source[side, :, block * 2 * TILE : (block + 1) * 2 * TILE], 2 * block)
                packed = jnp.where(wide_row // 2 == block, value, packed)
            target[side] = packed

    messages = (
        (go_right, from_left),
        (go_left, from_right),
        (go_right_two, from_left_two),
        (go_left_two, from_right_two),
    )

    def halo_copy(n, side, slot, device, block=None):
        source, target = messages[n][0].at[side], messages[n][1].at[slot]
        at = n
        if block is not None:
            lanes = pl.ds(pl.multiple_of(block * 2 * TILE, 2 * TILE), 2 * TILE)
            source, target = source.at[:, :, lanes], target.at[:, :, lanes]
            at = 4 + n * blocks + block
        return pltpu.make_async_remote_copy(
            src_ref=source,
            dst_ref=target,
            send_sem=halo_send.at[side, at],
            recv_sem=halo_recv.at[slot, at],
            device_id=device,
            device_id_type=MESH,
        )

    def halo_out(n, side, block=None):
        step = STEPS[n]
        if side is near:
            by_other = wraps(step) & (half == 1) & (step < 0)
            gx_to, gy_to = beside(step)
            return halo_copy(n, side, jnp.where(by_other, 3, side), (gx_to, jnp.where(by_other, other, gy_to)), block)
        return halo_copy(n, side, jnp.where(wraps(step), 2, side), nearest(step), block)

    def halo_in(n, side, block=None):
        return halo_copy(n, side, side, beside(STEPS[n]), block)

    def wrapped_in(n, side, block=None):
        return halo_copy(n, side, 2 if side is near else 3, beside(STEPS[n]), block)

    def block_from_here(i):
        column, back = gy // 4, blocks - 1 - i
        return lax.rem(column // 2 + back // 2, 2) * 2 + lax.rem(column + back, 2)

    came = [wraps(-step) for step in STEPS]
    straight = [jnp.logical_not(flag) for flag in came]

    def kept(side):
        return straight if side is far else [True, straight[1] | (half == 0), True, straight[3] | (half == 0)]

    def only(flag, value):
        if isinstance(flag, bool):
            return value if flag else 0.0
        return jnp.where(flag, value, 0.0)

    def unpack_two(slot, keep):
        tail = NAMES[("tail", 0)]
        tails = jnp.broadcast_to(table_ref[:, tail : tail + 1], (ROWS, 2 * TILE))
        for block in range(blocks):
            head = jnp.where(wide_row < 2, down(from_left_two[slot], ROWS - 2 * block), 0.0)
            late = from_right_two[slot]
            late = jnp.where(wide_row < 6, down(late, 4 - 2 * block), down(late, 6 - 2 * block))
            tail_two[slot, :, block * 2 * TILE : (block + 1) * 2 * TILE] = only(keep[2], head) + only(keep[3], tails * late)

    def spread_rows(a, b):
        return [jnp.where(low_row, a, down(b, 4)), jnp.where(low_row, down(a, 4), b)]

    def halo_tiles(slot, keep, here):
        tiles = []
        for pair in range(2):
            tiles += spread_rows(only(keep[0], from_left[slot, pair, :, here]), only(keep[1], from_right[slot, pair, :, here]))
        a, b = only(keep[0], from_left[slot, 2, :, here]), only(keep[1], from_right[slot, 2, :, here])
        return tiles + [tail_two[slot, :, here] + (a + b)]

    def lanes_of(block, core):
        return pl.ds(pl.multiple_of((block * 2 + core) * TILE, TILE), TILE)

    def combine(side, block, core, target, slot):
        here = lanes_of(block, core)
        tiles = halo_tiles(side, kept(side), here)
        for n in range(4):
            target[slot, n] = own[side, n, :, here] + tiles[n]
        target[slot, 4] = own_two[side, :, here] + tiles[4]

    def tile_copy(tile):
        return pltpu.make_async_remote_copy(
            src_ref=send.at[tile],
            dst_ref=got.at[gy],
            send_sem=send_sem.at[tile],
            recv_sem=recv_sem.at[gy],
            device_id=(gx, tile),
            device_id_type=MESH,
        )

    def arrival(tile):
        return pltpu.make_async_remote_copy(
            src_ref=send.at[tile],
            dst_ref=got.at[tile],
            send_sem=send_sem.at[tile],
            recv_sem=recv_sem.at[tile],
            device_id=(gx, tile),
            device_id_type=MESH,
        )

    x_pass(far)
    pack_two(far)
    late_greetings = jnp.where(wraps(1), 2, jnp.where(wraps(2), 1, 0)) * half
    late_greetings += jnp.where(wraps(-1), 2, jnp.where(wraps(-2), 1, 0)) * jnp.where(heard, 1, 0)
    near_first = (half == 0) | wraps(8) | wraps(-2)

    @pl.when(near_first)
    def _():
        x_pass(near)
        pack_two(near)

    pl.semaphore_wait(barrier, 5 + 2 * column + 2 * blocks * half + late_greetings)

    @pl.when(half == 1)
    def _():
        greet_far(go.at[column])

    def send_far_halos(n, condition):
        @pl.when(condition)
        def _():
            if n > 1:
                halo_out(n, far).start()
            else:
                @pl.loop(0, blocks)
                def _(i):
                    halo_out(n, far, block_from_here(i)).start()

    around = [wraps(step) for step in STEPS]
    for n in (2, 0):
        send_far_halos(n, around[n] & jnp.logical_not(answered[n]))
    for n in range(4):
        @pl.when(around[n])
        def _():
            halo_out(n, near).start()
    for n in (2, 3, 0, 1):
        send_far_halos(n, jnp.logical_not(around[n]) if STEPS[n] > 0 else gx >= 0)

    @pl.when(half == 1)
    def _():
        for n in (0, 2):
            @pl.when(answers[n])
            def _():
                pl.semaphore_signal(ready.at[n], inc=1, device_id=nearest(-STEPS[n]), device_id_type=MESH)

    signal_blocks(join, lambda block: column > block)

    @pl.when(jnp.logical_not(near_first))
    def _():
        x_pass(near)
        pack_two(near)

    late_near = (half == 1) & ((lax.rem(gx, 4) == 0) & (gx < 24)) | (gx == 23)

    def send_near_halos(flag):
        for n in range(4):
            @pl.when(flag & jnp.logical_not(wraps(STEPS[n])))
            def _():
                halo_out(n, near).start()

    send_near_halos(jnp.logical_not(late_near))

    def await_halos(numbers, side, block=None):
        for n in numbers:
            @pl.when(kept(side)[n])
            def _():
                halo_in(n, side, block).wait_recv()

    def relay_copy(slot, tile, count):
        return pltpu.make_async_remote_copy(
            src_ref=relay.at[tile, pl.ds(0, count)],
            dst_ref=relayed.at[slot, pl.ds(0, count)],
            send_sem=relay_send.at[tile],
            recv_sem=relay_recv.at[slot],
            device_id=(gx, tile),
            device_id_type=MESH,
        )

    def at_ends(act, *ends):
        for low in ends:
            for place, count in ((0, 3), (1, 1)):
                @pl.when(gx == (place if low else nx - 1 - place))
                def _():
                    act(low, count)

    def pass_on(side, low, count):
        ones, twos = (from_left, 2) if low else (from_right, 3)
        slot = 2 if side is near else 3

        def fill(block, core, target, place):
            here = lanes_of(block, core)
            value = tail_two[slot, :, here]
            if count == 3:
                target[place, 0] = value + ones[slot, 2, :, here]
                for pair in range(2):
                    target[place, 1 + pair] = ones[slot, pair, :, here]
            else:
                target[place, 0] = value

        wrapped_in(twos, side).wait_recv()
        if count == 3 and side is far:
            wrapped_in(twos - 2, side).wait_recv()
        elif count == 3:
            for block in range(blocks):
                wrapped_in(twos - 2, side, block).wait_recv()
        unpack_two(slot, [None, None, low, not low])

        @pl.loop(1 if side is near else 0, 2 * blocks)
        def _(j):
            block, core, tile = peer(side, j)
            fill(block, core, relay, tile)
            relay_copy(gy, tile, count).start()

        if side is near:
            fill(gy // 4, lax.rem(gy, 2), relayed, gy)

    await_halos((2, 3), far)
    unpack_two(far, kept(far))

    @pl.loop(0, blocks)
    def _(i):
        await_halos((0, 1), far, block_from_here(i))
        for j in range(2):
            block, core = block_from_here(i), lax.rem(gy + j, 2)
            tile = block * 4 + far * 2 + core
            combine(far, block, core, send, tile)

            @pl.when(half == 1)
            def _():
                tile_copy(tile).start()

    send_near_halos(late_near)

    for n in (0, 2):
        @pl.when(answered[n])
        def _():
            pl.semaphore_wait(ready.at[n], 1)
        send_far_halos(n, answered[n])

    @pl.when(half == 0)
    def _():
        @pl.loop(0, blocks)
        def _(block):
            pl.semaphore_wait(go.at[block], 2)
            for core in range(2):
                tile_copy(block * 4 + far * 2 + core).start()

        at_ends(functools.partial(pass_on, far), False)

    await_halos(range(4), near)
    unpack_two(near, kept(near))
    @pl.when(column < blocks - 1)
    def _():
        pl.semaphore_wait(join, 2 * (blocks - 1 - column))

    @pl.loop(1, 2 * blocks)
    def _(j):
        block, core, tile = peer(near, j)
        combine(near, block, core, send, tile)
        tile_copy(tile).start()

    combine(near, gy // 4, lax.rem(gy, 2), got, gy)

    at_ends(functools.partial(pass_on, near), True, False)


    @pl.loop(1, 2 * blocks)
    def _(j):
        arrival(peer(near, j)[2]).wait_recv()

    @pl.loop(0, 2 * blocks)
    def _(j):
        arrival(peer(far, j)[2]).wait_recv()

    def take_over(low, count):
        def take(side, first, back):
            @pl.loop(first, 2 * blocks)
            def _(j):
                tile = peer(side, j)[2]
                relay_copy(tile, tile, count).wait_recv()

            @pl.loop(0, 2 * blocks)
            def _(j):
                tile, owner = peer(side, j)[2], peer(back, j)[2]
                if count == 3:
                    for pair in range(2):
                        value = relayed[tile, 1 + pair]
                        for n, rows in enumerate(spread_rows(value, 0.0) if low else spread_rows(0.0, value)):
                            got[owner, 2 * pair + n] += rows
                got[owner, 4] += relayed[tile, 0]

        take(near, 1, far)
        if not low:
            @pl.when(half == 1)
            def _():
                take(far, 0, near)

    at_ends(take_over, True, False)

    for n in range(4):
        halo_out(n, near).wait_send()
    for n in (2, 3):
        halo_out(n, far).wait_send()

    @pl.loop(0, blocks)
    def _(i):
        for n in (0, 1):
            halo_out(n, far, block_from_here(i)).wait_send()

    @pl.loop(1, 2 * blocks)
    def _(j):
        tile_copy(peer(near, j)[2]).wait_send()

    @pl.loop(0, 2 * blocks)
    def _(j):
        tile_copy(peer(far, j)[2]).wait_send()

    def drain(low, count):
        @pl.loop(1, 2 * blocks)
        def _(j):
            relay_copy(gy, peer(near, j)[2], count).wait_send()

        if not low:
            @pl.when(half == 0)
            def _():
                @pl.loop(0, 2 * blocks)
                def _(j):
                    relay_copy(gy, peer(far, j)[2], count).wait_send()

    at_ends(drain, True, False)


def z_kernel(ny, got, out_hbm, out_ref, sems):
    pairs = 2 * ny
    shape = (pairs, ROWS, TILE)
    wide = lax.broadcasted_iota(jnp.int32, (ny, ROWS, TILE), 2) % 2 == 0
    pairs_one = [swap(got[:, n], got[:, n + 1], wide, 1, 2) for n in (0, 2)]
    s, r = leading_lift(*(jnp.stack(both, axis=1).reshape(shape) for both in zip(*pairs_one)))
    out_ref[1] = r
    odd_copy = pltpu.make_async_copy(out_ref.at[1], out_hbm.at[:, 1], sems.at[1])
    odd_copy.start()
    slot = got[:, 4]
    under = pltpu.roll(slot, ROWS - 1, 1)

    def left(value):
        return pltpu.roll(value, TILE - 1, 2)

    even = jnp.stack([slot, under], axis=1).reshape(shape)
    odd = jnp.stack([left(slot), left(under)], axis=1).reshape(shape)
    coarse = leading_lift(even, odd)[0].reshape(ny, 2, ROWS, TILE)
    low, high = leading_lift(coarse[:, 0], coarse[:, 1])
    coarse = jnp.stack([low, high], axis=1).reshape(shape)
    corner = (lax.broadcasted_iota(jnp.int32, shape, 1) % 2 == 0) & (lax.broadcasted_iota(jnp.int32, shape, 2) % 2 == 0)
    out_ref[0] = jnp.where(corner, coarse, s)
    even_copy = pltpu.make_async_copy(out_ref.at[0], out_hbm.at[:, 0], sems.at[0])
    even_copy.start()
    odd_copy.wait()
    even_copy.wait()


def solution(mesh):
    nx, ny = mesh.shape["gx"], mesh.shape["gy"]
    length = ny * TILE
    half = length // 2

    def body(velocity):
        got = pl.pallas_call(
            functools.partial(kernel, nx, ny),
            out_shape=jax.ShapeDtypeStruct((ny, 5, ROWS, TILE), F32),
            in_specs=[pl.BlockSpec(memory_space=pl.ANY)] * 2,
            out_specs=pl.BlockSpec(memory_space=pltpu.VMEM),
            scratch_shapes=[
                pltpu.VMEM((4, ROWS, length), F32),
                pltpu.VMEM((ROWS, TILE), F32),
                pltpu.VMEM((len(NAMES), ROWS, TILE), F32),
                pltpu.VMEM((4, ROWS, length), F32),
                pltpu.VMEM((2, ROWS, length), F32),
                pltpu.VMEM((2, 4, ROWS, half), F32),
                pltpu.VMEM((2, ROWS, half), F32),
                pltpu.VMEM((2, ROWS, half), F32),
                pltpu.VMEM((2, ROWS, half), F32),
                pltpu.VMEM((2, 3, ROWS, half), F32),
                pltpu.VMEM((2, 3, ROWS, half), F32),
                pltpu.VMEM((2, ROWS, 2 * TILE), F32),
                pltpu.VMEM((2, ROWS, 2 * TILE), F32),
                pltpu.VMEM((4, 3, ROWS, half), F32),
                pltpu.VMEM((4, 3, ROWS, half), F32),
                pltpu.VMEM((4, ROWS, 2 * TILE), F32),
                pltpu.VMEM((4, ROWS, 2 * TILE), F32),
                pltpu.VMEM((4, ROWS, half), F32),
                pltpu.VMEM((ny, 5, ROWS, TILE), F32),
                pltpu.VMEM((ny, 3, ROWS, TILE), F32),
                pltpu.VMEM((ny, 3, ROWS, TILE), F32),
                pltpu.SemaphoreType.DMA((3,)),
                pltpu.SemaphoreType.DMA((2, 4 + ny // 2)),
                pltpu.SemaphoreType.DMA((4, 4 + ny // 2)),
                pltpu.SemaphoreType.DMA((ny,)),
                pltpu.SemaphoreType.DMA((ny,)),
                pltpu.SemaphoreType.DMA((ny,)),
                pltpu.SemaphoreType.DMA((ny,)),
                pltpu.SemaphoreType.REGULAR((ny // 4,)),
                pltpu.SemaphoreType.REGULAR((4,)),
                pltpu.SemaphoreType.REGULAR,
            ],
            compiler_params=pltpu.CompilerParams(collective_id=0, has_side_effects=True, vmem_limit_bytes=24576 * 1024),
        )(pltpu.with_memory_space_constraint(velocity, pltpu.HBM), pltpu.with_memory_space_constraint(jnp.asarray(COLUMNS), pltpu.HBM))
        out = pl.pallas_call(
            functools.partial(z_kernel, ny),
            out_shape=jax.ShapeDtypeStruct((2 * ny, 2, ROWS, TILE), F32),
            in_specs=[pl.BlockSpec(memory_space=pltpu.VMEM)],
            out_specs=pl.BlockSpec(memory_space=pl.ANY),
            scratch_shapes=[pltpu.VMEM((2, 2 * ny, ROWS, TILE), F32), pltpu.SemaphoreType.DMA((2,))],
            compiler_params=pltpu.CompilerParams(vmem_limit_bytes=24 * 2**20),
        )(got)
        return out.reshape(4 * ny, ROWS, TILE)

    return jax.shard_map(
        body, mesh=mesh, in_specs=(P("gy", "gx", None),), out_specs=P(None, "gx", "gy"), check_vma=False
    )
```

```python
import functools

import jax
import jax.numpy as jnp
import numpy as np
from jax import lax
from jax.experimental import pallas as pl
from jax.experimental.pallas import tpu as pltpu
from jax.sharding import PartitionSpec as P

PREDICT_FIRST = -1.586134342
UPDATE_FIRST = -0.05298011854
PREDICT_SECOND = 0.8829110762
UPDATE_SECOND = 0.4435068522
SCALE_LOW = 1.149604398
SCALE_HIGH = 1.0 / 1.149604398

MESH = pl.DeviceIdType.MESH
ROWS = 8
STEPS = (1, -1, 2, -2)
TILE = 128
F32 = jnp.float32


def lift_matrix(extent):
    table = np.eye(extent)
    s, r = table[0::2], table[1::2]
    r = r + PREDICT_FIRST * (s + np.roll(s, -1, 0))
    s = s + UPDATE_FIRST * (r + np.roll(r, 1, 0))
    r = r + PREDICT_SECOND * (s + np.roll(s, -1, 0))
    s = s + UPDATE_SECOND * (r + np.roll(r, 1, 0))
    out = np.empty((extent, extent))
    out[0::2], out[1::2] = s * SCALE_LOW, r * SCALE_HIGH
    return out


LOW_TAPS = [float(tap) for tap in lift_matrix(32)[16, 16:21]]
HIGH_TAPS = [float(tap) for tap in lift_matrix(32)[17, 17:21]]


def row_operators():
    extent, mine = 128, 64
    first = lift_matrix(extent)
    second = lift_matrix(extent // 2) @ first[0::2]
    wide = np.zeros((extent, extent))
    wide[0::2] = second

    def block(table, step):
        start = mine + ROWS * step
        return table[start : start + ROWS, mine : mine + ROWS]

    return {step: block(first, step) for step in (-1, 0, 1)}, {step: block(wide, step) for step in (-2, -1, 0, 1, 2)}


def coefficient_columns():
    first, second = row_operators()
    columns, names = [], {}

    def add(name, column):
        if np.any(column != 0):
            names[name] = len(columns)
            columns.append(column)

    halo = first[1] + first[-1]
    assert not np.any((first[1] != 0) & (first[-1] != 0).any(axis=1, keepdims=True))
    even = np.arange(ROWS) // 2 * 2
    for j in range(ROWS):
        add(("own", j), first[0][:, j])
        add(("halo", j), halo[:, j])
        for step in (-1, 0, 1, 2):
            add((step, j), second[step][even, j])
    tail = np.zeros(ROWS)
    tail[4:] = second[-2][[4, 4, 6, 6], 0]
    add(("tail", 0), tail)
    table = np.zeros((ROWS, TILE), np.float32)
    table[:, : len(columns)] = np.stack(columns, 1)
    return table, names


COLUMNS, NAMES = coefficient_columns()


def lane_lift(s, r, stride):
    axis, length = s.ndim - 1, s.shape[-1]

    def at(a, pairs):
        return pltpu.roll(a, (-pairs * stride) % length, axis) if pairs else a

    low, high = LOW_TAPS, HIGH_TAPS
    s_next, s_last, r_next, r_last = at(s, 1), at(s, -1), at(r, 1), at(r, -1)
    s_after, s_before, r_before = at(s, 2), at(s, -2), at(r, -2)
    s_out = (low[0] * s + low[2] * (s_next + s_last)) + low[4] * (s_after + s_before)
    s_out = s_out + (low[1] * (r + r_last) + low[3] * (r_next + r_before))
    r_out = (high[0] * r + high[2] * (r_next + r_last)) + (high[1] * (s + s_next) + high[3] * (s_last + s_after))
    return s_out, r_out


def swap(a, b, low, stride, axis):
    size = a.shape[axis]
    return jnp.where(low, a, pltpu.roll(b, stride, axis)), jnp.where(low, pltpu.roll(a, size - stride, axis), b)


def leading_lift(s, r):
    def after(a):
        return jnp.concatenate([a[1:], a[:1]], axis=0)

    def before(a):
        return jnp.concatenate([a[-1:], a[:-1]], axis=0)

    r = r + PREDICT_FIRST * (s + after(s))
    s = s + UPDATE_FIRST * (r + before(r))
    r = r + PREDICT_SECOND * (s + after(s))
    s = s + UPDATE_SECOND * (r + before(r))
    return s * SCALE_LOW, r * SCALE_HIGH


def kernel(nx, ny, v_hbm, table_hbm, got, v_ref, table_ref, weights, y_one, y_two, own, own_two, far_two, near_two, go_right,
           go_left, go_right_two, go_left_two, from_left, from_right, from_left_two, from_right_two, tail_two, send,
           relay, relayed, in_sem, halo_send, halo_recv, send_sem, recv_sem, relay_send, relay_recv, go, ready, join):
    gx, gy = lax.axis_index("gx"), lax.axis_index("gy")
    half = (gy // 2) % 2
    blocks = ny // 4

    loads = [pltpu.make_async_copy(v_hbm.at[pl.ds(2 * pair, 2)], v_ref.at[pl.ds(2 * pair, 2)], in_sem.at[pair]) for pair in range(2)]
    load_table = pltpu.make_async_copy(table_hbm, table_ref, in_sem.at[2])
    loads[0].start()
    load_table.start()
    loads[1].start()

    other = gy + 2 - 4 * half

    def wraps(step):
        return jnp.logical_or(gx + step < 0, gx + step >= nx)

    def beside(step):
        return (lax.rem(gx + step + nx, nx), gy)

    def nearest(step):
        return (lax.rem(gx + step + nx, nx), jnp.where(wraps(step), other, gy))

    def peer(side, j):
        block = lax.rem(gy // 4 + j // 2, blocks)
        core = lax.rem(gy + j, 2)
        return block, core, block * 4 + side * 2 + core

    barrier = pltpu.get_barrier_semaphore()
    far, near = 1 - half, half
    answered = [wraps(step) & (half == 0) if step > 0 else gx < 0 for step in STEPS]
    answers = [wraps(-step) & (half == 1) if step > 0 else gx < 0 for step in STEPS]
    for n in range(4):
        back = (1, 0, 3, 2)[n]

        @pl.when(jnp.logical_not(answers[back]))
        def _():
            pl.semaphore_signal(barrier, inc=1, device_id=nearest(STEPS[n]), device_id_type=MESH)
    column = gy // 4
    pl.semaphore_signal(barrier, inc=1, device_id=(gx, peer(near, 1)[2]), device_id_type=MESH)

    def signal_blocks(semaphore, flag):
        for block in range(blocks):
            @pl.when(flag(block))
            def _():
                for core in range(2):
                    tile = block * 4 + near * 2 + core
                    pl.semaphore_signal(semaphore, inc=1, device_id=(gx, tile), device_id_type=MESH)

    signal_blocks(barrier, lambda block: column < block)

    def greet_far(semaphore):
        for j in range(2 * blocks):
            pl.semaphore_signal(semaphore, inc=1, device_id=(gx, peer(far, j)[2]), device_id_type=MESH)

    heard = (half == 0)
    for n in range(4):
        @pl.when(wraps(-STEPS[n]) & (heard if STEPS[n] < 0 else gx >= 0))
        def _():
            pl.semaphore_signal(barrier, inc=1, device_id=beside(-STEPS[n]), device_id_type=MESH)

    @pl.when(half == 0)
    def _():
        greet_far(barrier)

    load_table.wait()
    for at in range(len(NAMES)):
        weights[at] = jnp.broadcast_to(table_ref[:, at : at + 1], (ROWS, TILE))

    lane = lax.broadcasted_iota(jnp.int32, (ROWS, TILE), 1)
    row = lax.broadcasted_iota(jnp.int32, (ROWS, TILE), 0)
    low_row = row < 4
    even_row = row % 2 == 0

    def low_lanes(stride):
        return jnp.concatenate([(lane // stride) % 2] * ny, axis=1) == 0

    lows = []
    for pair in range(2):
        loads[pair].wait()
        s, r = swap(v_ref[2 * pair], v_ref[2 * pair + 1], low_lanes(1), 1, 1)
        s, r = lane_lift(s, r, 2)
        y_one[2 * pair] = s
        y_one[2 * pair + 1] = r
        lows.append(s)
    s, r = lane_lift(*swap(*lows, low_lanes(2), 2, 1), 4)
    y_two[0], y_two[1] = swap(s, r, low_lanes(2), 2, 1)

    def weigh(total, name, value):
        if name not in NAMES:
            return total
        term = weights[NAMES[name]] * value
        return term if total is None else total + term

    def down(value, k):
        return value if k % ROWS == 0 or isinstance(value, float) else pltpu.roll(value, k % ROWS, 0)

    def x_pass(side):
        @pl.loop(0, 2 * blocks)
        def _(p):
            tile = (p // 2) * 4 + side * 2 + p % 2
            lanes = pl.ds(pl.multiple_of(tile * TILE, TILE), TILE)
            here = pl.ds(pl.multiple_of(p * TILE, TILE), TILE)

            def spread(ref, z, j):
                return jnp.broadcast_to(ref[z, j : j + 1, lanes], (ROWS, TILE))

            mine, halos = [None] * 4, [None] * 4
            for j in range(ROWS):
                for z in range(4):
                    value = spread(y_one, z, j)
                    mine[z] = weigh(mine[z], ("own", j), value)
                    halos[z] = weigh(halos[z], ("halo", j), value)
            for z in range(4):
                own[side, z, :, here] = mine[z]
            for pair in range(2):
                a, b = halos[2 * pair], halos[2 * pair + 1]
                go_right[side, pair, :, here] = jnp.where(low_row, a, down(b, 4))
                go_left[side, pair, :, here] = jnp.where(low_row, down(a, 4), b)
            sums = {step: None for step in (-1, 0, 1, 2)}
            for j in range(ROWS):
                value = jnp.where(even_row, spread(y_two, 0, j), spread(y_two, 1, j))
                if j == 0:
                    near_two[side, :, here] = value
                for step in sums:
                    sums[step] = weigh(sums[step], (step, j), value)
            own_two[side, :, here] = sums[0]
            go_right[side, 2, :, here] = sums[1]
            go_left[side, 2, :, here] = sums[-1]
            far_two[side, :, here] = sums[2]

    wide_row = lax.broadcasted_iota(jnp.int32, (ROWS, 2 * TILE), 0)

    def pack_two(side):
        for source, target in ((far_two, go_right_two), (near_two, go_left_two)):
            packed = source[side, :, 0 : 2 * TILE]
            for block in range(1, blocks):
                value = down(source[side, :, block * 2 * TILE : (block + 1) * 2 * TILE], 2 * block)
                packed = jnp.where(wide_row // 2 == block, value, packed)
            target[side] = packed

    messages = (
        (go_right, from_left),
        (go_left, from_right),
        (go_right_two, from_left_two),
        (go_left_two, from_right_two),
    )

    def halo_copy(n, side, slot, device, block=None):
        source, target = messages[n][0].at[side], messages[n][1].at[slot]
        at = n
        if block is not None:
            lanes = pl.ds(pl.multiple_of(block * 2 * TILE, 2 * TILE), 2 * TILE)
            source, target = source.at[:, :, lanes], target.at[:, :, lanes]
            at = 4 + n * blocks + block
        return pltpu.make_async_remote_copy(
            src_ref=source,
            dst_ref=target,
            send_sem=halo_send.at[side, at],
            recv_sem=halo_recv.at[slot, at],
            device_id=device,
            device_id_type=MESH,
        )

    def halo_out(n, side, block=None):
        step = STEPS[n]
        if side is near:
            by_other = wraps(step) & (half == 1) & (step < 0)
            gx_to, gy_to = beside(step)
            return halo_copy(n, side, jnp.where(by_other, 3, side), (gx_to, jnp.where(by_other, other, gy_to)), block)
        return halo_copy(n, side, jnp.where(wraps(step), 2, side), nearest(step), block)

    def halo_in(n, side, block=None):
        return halo_copy(n, side, side, beside(STEPS[n]), block)

    def wrapped_in(n, side, block=None):
        return halo_copy(n, side, 2 if side is near else 3, beside(STEPS[n]), block)

    def block_from_here(i):
        column, back = gy // 4, blocks - 1 - i
        return lax.rem(column // 2 + back // 2, 2) * 2 + lax.rem(column + back, 2)

    came = [wraps(-step) for step in STEPS]
    straight = [jnp.logical_not(flag) for flag in came]

    def kept(side):
        return straight if side is far else [True, straight[1] | (half == 0), True, straight[3] | (half == 0)]

    def only(flag, value):
        if isinstance(flag, bool):
            return value if flag else 0.0
        return jnp.where(flag, value, 0.0)

    def unpack_two(slot, keep):
        tail = NAMES[("tail", 0)]
        tails = jnp.broadcast_to(table_ref[:, tail : tail + 1], (ROWS, 2 * TILE))
        for block in range(blocks):
            head = jnp.where(wide_row < 2, down(from_left_two[slot], ROWS - 2 * block), 0.0)
            late = from_right_two[slot]
            late = jnp.where(wide_row < 6, down(late, 4 - 2 * block), down(late, 6 - 2 * block))
            tail_two[slot, :, block * 2 * TILE : (block + 1) * 2 * TILE] = only(keep[2], head) + only(keep[3], tails * late)

    def spread_rows(a, b):
        return [jnp.where(low_row, a, down(b, 4)), jnp.where(low_row, down(a, 4), b)]

    def halo_tiles(slot, keep, here):
        tiles = []
        for pair in range(2):
            tiles += spread_rows(only(keep[0], from_left[slot, pair, :, here]), only(keep[1], from_right[slot, pair, :, here]))
        a, b = only(keep[0], from_left[slot, 2, :, here]), only(keep[1], from_right[slot, 2, :, here])
        return tiles + [tail_two[slot, :, here] + (a + b)]

    def lanes_of(block, core):
        return pl.ds(pl.multiple_of((block * 2 + core) * TILE, TILE), TILE)

    def combine(side, block, core, target, slot):
        here = lanes_of(block, core)
        tiles = halo_tiles(side, kept(side), here)
        for n in range(4):
            target[slot, n] = own[side, n, :, here] + tiles[n]
        target[slot, 4] = own_two[side, :, here] + tiles[4]

    def tile_copy(tile):
        return pltpu.make_async_remote_copy(
            src_ref=send.at[tile],
            dst_ref=got.at[gy],
            send_sem=send_sem.at[tile],
            recv_sem=recv_sem.at[gy],
            device_id=(gx, tile),
            device_id_type=MESH,
        )

    def arrival(tile):
        return pltpu.make_async_remote_copy(
            src_ref=send.at[tile],
            dst_ref=got.at[tile],
            send_sem=send_sem.at[tile],
            recv_sem=recv_sem.at[tile],
            device_id=(gx, tile),
            device_id_type=MESH,
        )

    x_pass(far)
    pack_two(far)
    late_greetings = jnp.where(wraps(1), 2, jnp.where(wraps(2), 1, 0)) * half
    late_greetings += jnp.where(wraps(-1), 2, jnp.where(wraps(-2), 1, 0)) * jnp.where(heard, 1, 0)
    near_first = (half == 0) | wraps(8) | wraps(-2)

    @pl.when(near_first)
    def _():
        x_pass(near)
        pack_two(near)

    pl.semaphore_wait(barrier, 5 + 2 * column + 2 * blocks * half + late_greetings)

    @pl.when(half == 1)
    def _():
        greet_far(go.at[column])

    def send_far_halos(n, condition):
        @pl.when(condition)
        def _():
            if n > 1:
                halo_out(n, far).start()
            else:
                @pl.loop(0, blocks)
                def _(i):
                    halo_out(n, far, block_from_here(i)).start()

    around = [wraps(step) for step in STEPS]
    for n in (2, 0):
        send_far_halos(n, around[n] & jnp.logical_not(answered[n]))
    for n in range(4):
        @pl.when(around[n])
        def _():
            halo_out(n, near).start()
    for n in (2, 3):
        send_far_halos(n, jnp.logical_not(around[n]) if STEPS[n] > 0 else gx >= 0)

    @pl.loop(0, blocks)
    def _(i):
        halo_out(1, far, block_from_here(i)).start()

        @pl.when(jnp.logical_not(around[0]))
        def _():
            halo_out(0, far, block_from_here(i)).start()

    @pl.when(half == 1)
    def _():
        for n in (0, 2):
            @pl.when(answers[n])
            def _():
                pl.semaphore_signal(ready.at[n], inc=1, device_id=nearest(-STEPS[n]), device_id_type=MESH)

    signal_blocks(join, lambda block: column > block)

    @pl.when(jnp.logical_not(near_first))
    def _():
        x_pass(near)
        pack_two(near)

    late_near = (half == 1) & ((lax.rem(gx, 4) == 0) & (gx < 24)) | (gx == 23)

    def send_near_halos(flag):
        for n in range(4):
            @pl.when(flag & jnp.logical_not(wraps(STEPS[n])))
            def _():
                halo_out(n, near).start()

    send_near_halos(jnp.logical_not(late_near))

    def await_halos(numbers, side, block=None):
        for n in numbers:
            @pl.when(kept(side)[n])
            def _():
                halo_in(n, side, block).wait_recv()

    def relay_copy(slot, tile, count):
        return pltpu.make_async_remote_copy(
            src_ref=relay.at[tile, pl.ds(0, count)],
            dst_ref=relayed.at[slot, pl.ds(0, count)],
            send_sem=relay_send.at[tile],
            recv_sem=relay_recv.at[slot],
            device_id=(gx, tile),
            device_id_type=MESH,
        )

    def at_ends(act, *ends):
        for low in ends:
            for place, count in ((0, 3), (1, 1)):
                @pl.when(gx == (place if low else nx - 1 - place))
                def _():
                    act(low, count)

    def pass_on(side, low, count):
        ones, twos = (from_left, 2) if low else (from_right, 3)
        slot = 2 if side is near else 3

        def fill(block, core, target, place):
            here = lanes_of(block, core)
            value = tail_two[slot, :, here]
            if count == 3:
                target[place, 0] = value + ones[slot, 2, :, here]
                for pair in range(2):
                    target[place, 1 + pair] = ones[slot, pair, :, here]
            else:
                target[place, 0] = value

        wrapped_in(twos, side).wait_recv()
        if count == 3 and side is far:
            wrapped_in(twos - 2, side).wait_recv()
        elif count == 3:
            for block in range(blocks):
                wrapped_in(twos - 2, side, block).wait_recv()
        unpack_two(slot, [None, None, low, not low])

        @pl.loop(1 if side is near else 0, 2 * blocks)
        def _(j):
            block, core, tile = peer(side, j)
            fill(block, core, relay, tile)
            relay_copy(gy, tile, count).start()

        if side is near:
            fill(gy // 4, lax.rem(gy, 2), relayed, gy)

    await_halos((2, 3), far)
    unpack_two(far, kept(far))

    @pl.loop(0, blocks)
    def _(i):
        await_halos((0, 1), far, block_from_here(i))
        for j in range(2):
            block, core = block_from_here(i), lax.rem(gy + j, 2)
            tile = block * 4 + far * 2 + core
            combine(far, block, core, send, tile)

            @pl.when(half == 1)
            def _():
                tile_copy(tile).start()

    send_near_halos(late_near)

    for n in (0, 2):
        @pl.when(answered[n])
        def _():
            pl.semaphore_wait(ready.at[n], 1)
        send_far_halos(n, answered[n])

    @pl.when(half == 0)
    def _():
        @pl.loop(0, blocks)
        def _(block):
            pl.semaphore_wait(go.at[block], 2)
            for core in range(2):
                tile_copy(block * 4 + far * 2 + core).start()

        at_ends(functools.partial(pass_on, far), False)

    await_halos(range(4), near)
    unpack_two(near, kept(near))
    @pl.when(column < blocks - 1)
    def _():
        pl.semaphore_wait(join, 2 * (blocks - 1 - column))

    @pl.loop(1, 2 * blocks)
    def _(j):
        block, core, tile = peer(near, j)
        combine(near, block, core, send, tile)
        tile_copy(tile).start()

    combine(near, gy // 4, lax.rem(gy, 2), got, gy)

    at_ends(functools.partial(pass_on, near), True, False)


    @pl.loop(1, 2 * blocks)
    def _(j):
        arrival(peer(near, j)[2]).wait_recv()

    @pl.loop(0, 2 * blocks)
    def _(j):
        arrival(peer(far, j)[2]).wait_recv()

    def take_over(low, count):
        def take(side, first, back):
            @pl.loop(first, 2 * blocks)
            def _(j):
                tile = peer(side, j)[2]
                relay_copy(tile, tile, count).wait_recv()

            @pl.loop(0, 2 * blocks)
            def _(j):
                tile, owner = peer(side, j)[2], peer(back, j)[2]
                if count == 3:
                    for pair in range(2):
                        value = relayed[tile, 1 + pair]
                        for n, rows in enumerate(spread_rows(value, 0.0) if low else spread_rows(0.0, value)):
                            got[owner, 2 * pair + n] += rows
                got[owner, 4] += relayed[tile, 0]

        take(near, 1, far)
        if not low:
            @pl.when(half == 1)
            def _():
                take(far, 0, near)

    at_ends(take_over, True, False)

    for n in range(4):
        halo_out(n, near).wait_send()
    for n in (2, 3):
        halo_out(n, far).wait_send()

    @pl.loop(0, blocks)
    def _(i):
        for n in (0, 1):
            halo_out(n, far, block_from_here(i)).wait_send()

    @pl.loop(1, 2 * blocks)
    def _(j):
        tile_copy(peer(near, j)[2]).wait_send()

    @pl.loop(0, 2 * blocks)
    def _(j):
        tile_copy(peer(far, j)[2]).wait_send()

    def drain(low, count):
        @pl.loop(1, 2 * blocks)
        def _(j):
            relay_copy(gy, peer(near, j)[2], count).wait_send()

        if not low:
            @pl.when(half == 0)
            def _():
                @pl.loop(0, 2 * blocks)
                def _(j):
                    relay_copy(gy, peer(far, j)[2], count).wait_send()

    at_ends(drain, True, False)


def z_kernel(ny, got, out_hbm, out_ref, sems):
    pairs = 2 * ny
    shape = (pairs, ROWS, TILE)
    wide = lax.broadcasted_iota(jnp.int32, (ny, ROWS, TILE), 2) % 2 == 0
    pairs_one = [swap(got[:, n], got[:, n + 1], wide, 1, 2) for n in (0, 2)]
    s, r = leading_lift(*(jnp.stack(both, axis=1).reshape(shape) for both in zip(*pairs_one)))
    out_ref[1] = r
    odd_copy = pltpu.make_async_copy(out_ref.at[1], out_hbm.at[:, 1], sems.at[1])
    odd_copy.start()
    slot = got[:, 4]
    under = pltpu.roll(slot, ROWS - 1, 1)

    def left(value):
        return pltpu.roll(value, TILE - 1, 2)

    even = jnp.stack([slot, under], axis=1).reshape(shape)
    odd = jnp.stack([left(slot), left(under)], axis=1).reshape(shape)
    coarse = leading_lift(even, odd)[0].reshape(ny, 2, ROWS, TILE)
    low, high = leading_lift(coarse[:, 0], coarse[:, 1])
    coarse = jnp.stack([low, high], axis=1).reshape(shape)
    corner = (lax.broadcasted_iota(jnp.int32, shape, 1) % 2 == 0) & (lax.broadcasted_iota(jnp.int32, shape, 2) % 2 == 0)
    out_ref[0] = jnp.where(corner, coarse, s)
    even_copy = pltpu.make_async_copy(out_ref.at[0], out_hbm.at[:, 0], sems.at[0])
    even_copy.start()
    odd_copy.wait()
    even_copy.wait()


def solution(mesh):
    nx, ny = mesh.shape["gx"], mesh.shape["gy"]
    length = ny * TILE
    half = length // 2

    def body(velocity):
        got = pl.pallas_call(
            functools.partial(kernel, nx, ny),
            out_shape=jax.ShapeDtypeStruct((ny, 5, ROWS, TILE), F32),
            in_specs=[pl.BlockSpec(memory_space=pl.ANY)] * 2,
            out_specs=pl.BlockSpec(memory_space=pltpu.VMEM),
            scratch_shapes=[
                pltpu.VMEM((4, ROWS, length), F32),
                pltpu.VMEM((ROWS, TILE), F32),
                pltpu.VMEM((len(NAMES), ROWS, TILE), F32),
                pltpu.VMEM((4, ROWS, length), F32),
                pltpu.VMEM((2, ROWS, length), F32),
                pltpu.VMEM((2, 4, ROWS, half), F32),
                pltpu.VMEM((2, ROWS, half), F32),
                pltpu.VMEM((2, ROWS, half), F32),
                pltpu.VMEM((2, ROWS, half), F32),
                pltpu.VMEM((2, 3, ROWS, half), F32),
                pltpu.VMEM((2, 3, ROWS, half), F32),
                pltpu.VMEM((2, ROWS, 2 * TILE), F32),
                pltpu.VMEM((2, ROWS, 2 * TILE), F32),
                pltpu.VMEM((4, 3, ROWS, half), F32),
                pltpu.VMEM((4, 3, ROWS, half), F32),
                pltpu.VMEM((4, ROWS, 2 * TILE), F32),
                pltpu.VMEM((4, ROWS, 2 * TILE), F32),
                pltpu.VMEM((4, ROWS, half), F32),
                pltpu.VMEM((ny, 5, ROWS, TILE), F32),
                pltpu.VMEM((ny, 3, ROWS, TILE), F32),
                pltpu.VMEM((ny, 3, ROWS, TILE), F32),
                pltpu.SemaphoreType.DMA((3,)),
                pltpu.SemaphoreType.DMA((2, 4 + ny // 2)),
                pltpu.SemaphoreType.DMA((4, 4 + ny // 2)),
                pltpu.SemaphoreType.DMA((ny,)),
                pltpu.SemaphoreType.DMA((ny,)),
                pltpu.SemaphoreType.DMA((ny,)),
                pltpu.SemaphoreType.DMA((ny,)),
                pltpu.SemaphoreType.REGULAR((ny // 4,)),
                pltpu.SemaphoreType.REGULAR((4,)),
                pltpu.SemaphoreType.REGULAR,
            ],
            compiler_params=pltpu.CompilerParams(collective_id=0, has_side_effects=True, vmem_limit_bytes=24576 * 1024),
        )(pltpu.with_memory_space_constraint(velocity, pltpu.HBM), pltpu.with_memory_space_constraint(jnp.asarray(COLUMNS), pltpu.HBM))
        out = pl.pallas_call(
            functools.partial(z_kernel, ny),
            out_shape=jax.ShapeDtypeStruct((2 * ny, 2, ROWS, TILE), F32),
            in_specs=[pl.BlockSpec(memory_space=pltpu.VMEM)],
            out_specs=pl.BlockSpec(memory_space=pl.ANY),
            scratch_shapes=[pltpu.VMEM((2, 2 * ny, ROWS, TILE), F32), pltpu.SemaphoreType.DMA((2,))],
            compiler_params=pltpu.CompilerParams(vmem_limit_bytes=24 * 2**20),
        )(got)
        return out.reshape(4 * ny, ROWS, TILE)

    return jax.shard_map(
        body, mesh=mesh, in_specs=(P("gy", "gx", None),), out_specs=P(None, "gx", "gy"), check_vma=False
    )
```

```python
import functools

import jax
import jax.numpy as jnp
import numpy as np
from jax import lax
from jax.experimental import pallas as pl
from jax.experimental.pallas import tpu as pltpu
from jax.sharding import PartitionSpec as P

PREDICT_FIRST = -1.586134342
UPDATE_FIRST = -0.05298011854
PREDICT_SECOND = 0.8829110762
UPDATE_SECOND = 0.4435068522
SCALE_LOW = 1.149604398
SCALE_HIGH = 1.0 / 1.149604398

MESH = pl.DeviceIdType.MESH
ROWS = 8
STEPS = (1, -1, 2, -2)
TILE = 128
F32 = jnp.float32


def lift_matrix(extent):
    table = np.eye(extent)
    s, r = table[0::2], table[1::2]
    r = r + PREDICT_FIRST * (s + np.roll(s, -1, 0))
    s = s + UPDATE_FIRST * (r + np.roll(r, 1, 0))
    r = r + PREDICT_SECOND * (s + np.roll(s, -1, 0))
    s = s + UPDATE_SECOND * (r + np.roll(r, 1, 0))
    out = np.empty((extent, extent))
    out[0::2], out[1::2] = s * SCALE_LOW, r * SCALE_HIGH
    return out


LOW_TAPS = [float(tap) for tap in lift_matrix(32)[16, 16:21]]
HIGH_TAPS = [float(tap) for tap in lift_matrix(32)[17, 17:21]]


def row_operators():
    extent, mine = 128, 64
    first = lift_matrix(extent)
    second = lift_matrix(extent // 2) @ first[0::2]
    wide = np.zeros((extent, extent))
    wide[0::2] = second

    def block(table, step):
        start = mine + ROWS * step
        return table[start : start + ROWS, mine : mine + ROWS]

    return {step: block(first, step) for step in (-1, 0, 1)}, {step: block(wide, step) for step in (-2, -1, 0, 1, 2)}


def coefficient_columns():
    first, second = row_operators()
    columns, names = [], {}

    def add(name, column):
        if np.any(column != 0):
            names[name] = len(columns)
            columns.append(column)

    halo = first[1] + first[-1]
    assert not np.any((first[1] != 0) & (first[-1] != 0).any(axis=1, keepdims=True))
    even = np.arange(ROWS) // 2 * 2
    for j in range(ROWS):
        add(("own", j), first[0][:, j])
        add(("halo", j), halo[:, j])
        for step in (-1, 0, 1, 2):
            add((step, j), second[step][even, j])
    tail = np.zeros(ROWS)
    tail[4:] = second[-2][[4, 4, 6, 6], 0]
    add(("tail", 0), tail)
    table = np.zeros((ROWS, TILE), np.float32)
    table[:, : len(columns)] = np.stack(columns, 1)
    return table, names


COLUMNS, NAMES = coefficient_columns()


def lane_lift(s, r, stride):
    axis, length = s.ndim - 1, s.shape[-1]

    def at(a, pairs):
        return pltpu.roll(a, (-pairs * stride) % length, axis) if pairs else a

    low, high = LOW_TAPS, HIGH_TAPS
    s_next, s_last, r_next, r_last = at(s, 1), at(s, -1), at(r, 1), at(r, -1)
    s_after, s_before, r_before = at(s, 2), at(s, -2), at(r, -2)
    s_out = (low[0] * s + low[2] * (s_next + s_last)) + low[4] * (s_after + s_before)
    s_out = s_out + (low[1] * (r + r_last) + low[3] * (r_next + r_before))
    r_out = (high[0] * r + high[2] * (r_next + r_last)) + (high[1] * (s + s_next) + high[3] * (s_last + s_after))
    return s_out, r_out


def swap(a, b, low, stride, axis):
    size = a.shape[axis]
    return jnp.where(low, a, pltpu.roll(b, stride, axis)), jnp.where(low, pltpu.roll(a, size - stride, axis), b)


def leading_lift(s, r):
    def after(a):
        return jnp.concatenate([a[1:], a[:1]], axis=0)

    def before(a):
        return jnp.concatenate([a[-1:], a[:-1]], axis=0)

    r = r + PREDICT_FIRST * (s + after(s))
    s = s + UPDATE_FIRST * (r + before(r))
    r = r + PREDICT_SECOND * (s + after(s))
    s = s + UPDATE_SECOND * (r + before(r))
    return s * SCALE_LOW, r * SCALE_HIGH


def kernel(nx, ny, v_hbm, table_hbm, out_ref, v_ref, table_ref, weights, y_one, y_two, own, own_two, far_two, near_two, go_right,
           go_left, go_right_two, go_left_two, from_left, from_right, from_left_two, from_right_two, tail_two, send, got,
           relay, relayed, in_sem, halo_send, halo_recv, send_sem, recv_sem, relay_send, relay_recv, go, ready, join):
    gx, gy = lax.axis_index("gx"), lax.axis_index("gy")
    half = (gy // 2) % 2
    blocks = ny // 4
    width = 2 * blocks * TILE

    loads = [pltpu.make_async_copy(v_hbm.at[pl.ds(2 * pair, 2)], v_ref.at[pl.ds(2 * pair, 2)], in_sem.at[pair]) for pair in range(2)]
    load_table = pltpu.make_async_copy(table_hbm, table_ref, in_sem.at[2])
    loads[0].start()
    load_table.start()
    loads[1].start()

    other = gy + 2 - 4 * half

    def wraps(step):
        return jnp.logical_or(gx + step < 0, gx + step >= nx)

    def beside(step):
        return (lax.rem(gx + step + nx, nx), gy)

    def nearest(step):
        return (lax.rem(gx + step + nx, nx), jnp.where(wraps(step), other, gy))

    def peer(side, j):
        block = lax.rem(gy // 4 + j // 2, blocks)
        core = lax.rem(gy + j, 2)
        return block, core, block * 4 + side * 2 + core

    barrier = pltpu.get_barrier_semaphore()
    far, near = 1 - half, half
    answered = [wraps(step) & (half == 0) if step > 0 else gx < 0 for step in STEPS]
    answers = [wraps(-step) & (half == 1) if step > 0 else gx < 0 for step in STEPS]
    for n in range(4):
        back = (1, 0, 3, 2)[n]

        @pl.when(jnp.logical_not(answers[back]))
        def _():
            pl.semaphore_signal(barrier, inc=1, device_id=nearest(STEPS[n]), device_id_type=MESH)
    column = gy // 4
    pl.semaphore_signal(barrier, inc=1, device_id=(gx, peer(near, 1)[2]), device_id_type=MESH)

    def signal_blocks(semaphore, flag):
        for block in range(blocks):
            @pl.when(flag(block))
            def _():
                for core in range(2):
                    tile = block * 4 + near * 2 + core
                    pl.semaphore_signal(semaphore, inc=1, device_id=(gx, tile), device_id_type=MESH)

    signal_blocks(barrier, lambda block: column < block)

    def greet_far(semaphore):
        for j in range(2 * blocks):
            pl.semaphore_signal(semaphore, inc=1, device_id=(gx, peer(far, j)[2]), device_id_type=MESH)

    heard = (half == 0)
    for n in range(4):
        @pl.when(wraps(-STEPS[n]) & (heard if STEPS[n] < 0 else gx >= 0))
        def _():
            pl.semaphore_signal(barrier, inc=1, device_id=beside(-STEPS[n]), device_id_type=MESH)

    @pl.when(half == 0)
    def _():
        greet_far(barrier)

    load_table.wait()
    for at in range(len(NAMES)):
        weights[at] = jnp.broadcast_to(table_ref[:, at : at + 1], (ROWS, TILE))

    lane = lax.broadcasted_iota(jnp.int32, (ROWS, TILE), 1)
    row = lax.broadcasted_iota(jnp.int32, (ROWS, TILE), 0)
    low_row = row < 4
    even_row = row % 2 == 0

    def low_lanes(stride):
        return jnp.concatenate([(lane // stride) % 2] * ny, axis=1) == 0

    lows = []
    for pair in range(2):
        loads[pair].wait()
        s, r = swap(v_ref[2 * pair], v_ref[2 * pair + 1], low_lanes(1), 1, 1)
        s, r = lane_lift(s, r, 2)
        y_one[2 * pair] = s
        y_one[2 * pair + 1] = r
        lows.append(s)
    s, r = lane_lift(*swap(*lows, low_lanes(2), 2, 1), 4)
    y_two[0], y_two[1] = swap(s, r, low_lanes(2), 2, 1)

    def weigh(total, name, value):
        if name not in NAMES:
            return total
        term = weights[NAMES[name]] * value
        return term if total is None else total + term

    def down(value, k):
        return value if k % ROWS == 0 or isinstance(value, float) else pltpu.roll(value, k % ROWS, 0)

    def x_pass(side):
        @pl.loop(0, 2 * blocks)
        def _(p):
            tile = (p // 2) * 4 + side * 2 + p % 2
            lanes = pl.ds(pl.multiple_of(tile * TILE, TILE), TILE)
            here = pl.ds(pl.multiple_of(p * TILE, TILE), TILE)

            def spread(ref, z, j):
                return jnp.broadcast_to(ref[z, j : j + 1, lanes], (ROWS, TILE))

            mine, halos = [None] * 4, [None] * 4
            for j in range(ROWS):
                for z in range(4):
                    value = spread(y_one, z, j)
                    mine[z] = weigh(mine[z], ("own", j), value)
                    halos[z] = weigh(halos[z], ("halo", j), value)
            for z in range(4):
                own[side, z, :, here] = mine[z]
            for pair in range(2):
                a, b = halos[2 * pair], halos[2 * pair + 1]
                go_right[side, pair, :, here] = jnp.where(low_row, a, down(b, 4))
                go_left[side, pair, :, here] = jnp.where(low_row, down(a, 4), b)
            sums = {step: None for step in (-1, 0, 1, 2)}
            for j in range(ROWS):
                value = jnp.where(even_row, spread(y_two, 0, j), spread(y_two, 1, j))
                if j == 0:
                    near_two[side, :, here] = value
                for step in sums:
                    sums[step] = weigh(sums[step], (step, j), value)
            own_two[side, :, here] = sums[0]
            go_right[side, 2, :, here] = sums[1]
            go_left[side, 2, :, here] = sums[-1]
            far_two[side, :, here] = sums[2]

    wide_row = lax.broadcasted_iota(jnp.int32, (ROWS, 2 * TILE), 0)

    def pack_two(side):
        for source, target in ((far_two, go_right_two), (near_two, go_left_two)):
            packed = source[side, :, 0 : 2 * TILE]
            for block in range(1, blocks):
                value = down(source[side, :, block * 2 * TILE : (block + 1) * 2 * TILE], 2 * block)
                packed = jnp.where(wide_row // 2 == block, value, packed)
            target[side] = packed

    messages = (
        (go_right, from_left),
        (go_left, from_right),
        (go_right_two, from_left_two),
        (go_left_two, from_right_two),
    )

    def halo_copy(n, side, slot, device, block=None):
        source, target = messages[n][0].at[side], messages[n][1].at[slot]
        at = n
        if block is not None:
            lanes = pl.ds(pl.multiple_of(block * 2 * TILE, 2 * TILE), 2 * TILE)
            source, target = source.at[:, :, lanes], target.at[:, :, lanes]
            at = 4 + n * blocks + block
        return pltpu.make_async_remote_copy(
            src_ref=source,
            dst_ref=target,
            send_sem=halo_send.at[side, at],
            recv_sem=halo_recv.at[slot, at],
            device_id=device,
            device_id_type=MESH,
        )

    def halo_out(n, side, block=None):
        step = STEPS[n]
        if side is near:
            by_other = wraps(step) & (half == 1) & (step < 0)
            gx_to, gy_to = beside(step)
            return halo_copy(n, side, jnp.where(by_other, 3, side), (gx_to, jnp.where(by_other, other, gy_to)), block)
        return halo_copy(n, side, jnp.where(wraps(step), 2, side), nearest(step), block)

    def halo_in(n, side, block=None):
        return halo_copy(n, side, side, beside(STEPS[n]), block)

    def wrapped_in(n, side, block=None):
        return halo_copy(n, side, 2 if side is near else 3, beside(STEPS[n]), block)

    def block_from_here(i):
        return lax.rem(gy // 4 + i, blocks)

    came = [wraps(-step) for step in STEPS]
    straight = [jnp.logical_not(flag) for flag in came]

    def kept(side):
        return straight if side is far else [True, straight[1] | (half == 0), True, straight[3] | (half == 0)]

    def only(flag, value):
        if isinstance(flag, bool):
            return value if flag else 0.0
        return jnp.where(flag, value, 0.0)

    def unpack_two(slot, keep):
        tail = NAMES[("tail", 0)]
        tails = jnp.broadcast_to(table_ref[:, tail : tail + 1], (ROWS, 2 * TILE))
        for block in range(blocks):
            head = jnp.where(wide_row < 2, down(from_left_two[slot], ROWS - 2 * block), 0.0)
            late = from_right_two[slot]
            late = jnp.where(wide_row < 6, down(late, 4 - 2 * block), down(late, 6 - 2 * block))
            tail_two[slot, :, block * 2 * TILE : (block + 1) * 2 * TILE] = only(keep[2], head) + only(keep[3], tails * late)

    def spread_rows(a, b):
        return [jnp.where(low_row, a, down(b, 4)), jnp.where(low_row, down(a, 4), b)]

    def halo_tiles(slot, keep, here):
        tiles = []
        for pair in range(2):
            tiles += spread_rows(only(keep[0], from_left[slot, pair, :, here]), only(keep[1], from_right[slot, pair, :, here]))
        a, b = only(keep[0], from_left[slot, 2, :, here]), only(keep[1], from_right[slot, 2, :, here])
        return tiles + [tail_two[slot, :, here] + (a + b)]

    def lanes_of(block, core):
        return pl.ds(pl.multiple_of((block * 2 + core) * TILE, TILE), TILE)

    def combine(side, block, core, target, slot):
        here = lanes_of(block, core)
        tiles = halo_tiles(side, kept(side), here)
        for n in range(4):
            target[slot, n] = own[side, n, :, here] + tiles[n]
        target[slot, 4] = own_two[side, :, here] + tiles[4]

    def tile_copy(tile):
        return pltpu.make_async_remote_copy(
            src_ref=send.at[tile],
            dst_ref=got.at[gy],
            send_sem=send_sem.at[tile],
            recv_sem=recv_sem.at[gy],
            device_id=(gx, tile),
            device_id_type=MESH,
        )

    def arrival(tile):
        return pltpu.make_async_remote_copy(
            src_ref=send.at[tile],
            dst_ref=got.at[tile],
            send_sem=send_sem.at[tile],
            recv_sem=recv_sem.at[tile],
            device_id=(gx, tile),
            device_id_type=MESH,
        )

    x_pass(far)
    pack_two(far)
    late_greetings = jnp.where(wraps(1), 2, jnp.where(wraps(2), 1, 0)) * half
    late_greetings += jnp.where(wraps(-1), 2, jnp.where(wraps(-2), 1, 0)) * jnp.where(heard, 1, 0)
    near_first = (half == 0) | wraps(8)

    @pl.when(near_first)
    def _():
        x_pass(near)
        pack_two(near)

    pl.semaphore_wait(barrier, 5 + 2 * column + 2 * blocks * half + late_greetings)

    @pl.when(half == 1)
    def _():
        greet_far(go.at[column])

    def send_far_halos(n, condition):
        @pl.when(condition)
        def _():
            if n > 1:
                halo_out(n, far).start()
            else:
                @pl.loop(0, blocks)
                def _(i):
                    halo_out(n, far, block_from_here(i)).start()

    around = [wraps(step) & (heard if step < 0 else gx >= 0) for step in STEPS]
    for n in (2, 0):
        send_far_halos(n, around[n] & jnp.logical_not(answered[n]))
    for n in range(4):
        @pl.when(around[n])
        def _():
            halo_out(n, near).start()
    for n in (2, 3, 0, 1):
        send_far_halos(n, jnp.logical_not(around[n]) if STEPS[n] > 0 else gx >= 0)

    @pl.when(half == 1)
    def _():
        for n in (0, 2):
            @pl.when(answers[n])
            def _():
                pl.semaphore_signal(ready.at[n], inc=1, device_id=nearest(-STEPS[n]), device_id_type=MESH)

    signal_blocks(join, lambda block: column > block)

    @pl.when(jnp.logical_not(near_first))
    def _():
        x_pass(near)
        pack_two(near)

    late_near = (half == 1) & (lax.rem(gx, 4) == 0) & (gx < 24)

    def send_near_halos(flag):
        for n in range(4):
            @pl.when(flag & (jnp.logical_not(wraps(STEPS[n])) | ((half == 1) & (STEPS[n] < 0))))
            def _():
                halo_out(n, near).start()

    send_near_halos(jnp.logical_not(late_near) | wraps(-2))

    def await_halos(numbers, side, block=None):
        for n in numbers:
            @pl.when(kept(side)[n])
            def _():
                halo_in(n, side, block).wait_recv()

    def relay_copy(slot, tile, count):
        return pltpu.make_async_remote_copy(
            src_ref=relay.at[tile, pl.ds(0, count)],
            dst_ref=relayed.at[slot, pl.ds(0, count)],
            send_sem=relay_send.at[tile],
            recv_sem=relay_recv.at[slot],
            device_id=(gx, tile),
            device_id_type=MESH,
        )

    def at_ends(act, *ends):
        for low in ends:
            for place, count in ((0, 3), (1, 1)):
                @pl.when(gx == (place if low else nx - 1 - place))
                def _():
                    act(low, count)

    def pass_on(side, low, count):
        ones, twos = (from_left, 2) if low else (from_right, 3)
        slot = 2 if side is near else 3

        def fill(block, core, target, place):
            here = lanes_of(block, core)
            value = tail_two[slot, :, here]
            if count == 3:
                target[place, 0] = value + ones[slot, 2, :, here]
                for pair in range(2):
                    target[place, 1 + pair] = ones[slot, pair, :, here]
            else:
                target[place, 0] = value

        wrapped_in(twos, side).wait_recv()
        if count == 3 and side is far:
            wrapped_in(twos - 2, side).wait_recv()
        elif count == 3:
            for block in range(blocks):
                wrapped_in(twos - 2, side, block).wait_recv()
        unpack_two(slot, [None, None, low, not low])

        @pl.loop(1 if side is near else 0, 2 * blocks)
        def _(j):
            block, core, tile = peer(side, j)
            fill(block, core, relay, tile)
            relay_copy(gy, tile, count).start()

        if side is near:
            fill(gy // 4, lax.rem(gy, 2), relayed, gy)

    await_halos((2, 3), far)
    unpack_two(far, kept(far))

    @pl.loop(0, blocks)
    def _(i):
        await_halos((0, 1), far, block_from_here(i))
        for j in range(2):
            block, core, tile = peer(far, 2 * i + j)
            combine(far, block, core, send, tile)

            @pl.when(half == 1)
            def _():
                tile_copy(tile).start()

    send_near_halos(late_near & jnp.logical_not(wraps(-2)))

    for n in (0, 2):
        @pl.when(answered[n])
        def _():
            pl.semaphore_wait(ready.at[n], 1)
        send_far_halos(n, answered[n])

    @pl.when(half == 0)
    def _():
        @pl.loop(0, blocks)
        def _(block):
            pl.semaphore_wait(go.at[block], 2)
            for core in range(2):
                tile_copy(block * 4 + far * 2 + core).start()

        at_ends(functools.partial(pass_on, far), False)

    await_halos(range(4), near)
    unpack_two(near, kept(near))
    @pl.when(column < blocks - 1)
    def _():
        pl.semaphore_wait(join, 2 * (blocks - 1 - column))

    @pl.loop(1, 2 * blocks)
    def _(j):
        block, core, tile = peer(near, j)
        combine(near, block, core, send, tile)
        tile_copy(tile).start()

    combine(near, gy // 4, lax.rem(gy, 2), got, gy)

    at_ends(functools.partial(pass_on, near), True, False)


    @pl.loop(1, 2 * blocks)
    def _(j):
        arrival(peer(near, j)[2]).wait_recv()

    @pl.loop(0, 2 * blocks)
    def _(j):
        arrival(peer(far, j)[2]).wait_recv()

    def take_over(low, count):
        def take(side, first, back):
            @pl.loop(first, 2 * blocks)
            def _(j):
                tile = peer(side, j)[2]
                relay_copy(tile, tile, count).wait_recv()

            @pl.loop(0, 2 * blocks)
            def _(j):
                tile, owner = peer(side, j)[2], peer(back, j)[2]
                if count == 3:
                    for pair in range(2):
                        value = relayed[tile, 1 + pair]
                        for n, rows in enumerate(spread_rows(value, 0.0) if low else spread_rows(0.0, value)):
                            got[owner, 2 * pair + n] += rows
                got[owner, 4] += relayed[tile, 0]

        take(near, 1, far)
        if not low:
            @pl.when(half == 1)
            def _():
                take(far, 0, near)

    at_ends(take_over, True, False)

    pairs = 2 * ny
    shape = (pairs, ROWS, TILE)
    wide = lax.broadcasted_iota(jnp.int32, (ny, ROWS, TILE), 2) % 2 == 0
    pairs_one = [swap(got[:, n], got[:, n + 1], wide, 1, 2) for n in (0, 2)]
    s, r = leading_lift(*(jnp.stack(both, axis=1).reshape(shape) for both in zip(*pairs_one)))
    slot = got[:, 4]
    under = pltpu.roll(slot, ROWS - 1, 1)

    def left(value):
        return pltpu.roll(value, TILE - 1, 2)

    even = jnp.stack([slot, under], axis=1).reshape(shape)
    odd = jnp.stack([left(slot), left(under)], axis=1).reshape(shape)
    coarse = leading_lift(even, odd)[0].reshape(ny, 2, ROWS, TILE)
    low, high = leading_lift(coarse[:, 0], coarse[:, 1])
    coarse = jnp.stack([low, high], axis=1).reshape(shape)
    corner = (lax.broadcasted_iota(jnp.int32, shape, 1) % 2 == 0) & (lax.broadcasted_iota(jnp.int32, shape, 2) % 2 == 0)
    out_ref[:, 0] = jnp.where(corner, coarse, s)
    out_ref[:, 1] = r

    for n in range(4):
        halo_out(n, near).wait_send()
    for n in (2, 3):
        halo_out(n, far).wait_send()

    @pl.loop(0, blocks)
    def _(i):
        for n in (0, 1):
            halo_out(n, far, block_from_here(i)).wait_send()

    @pl.loop(1, 2 * blocks)
    def _(j):
        tile_copy(peer(near, j)[2]).wait_send()

    @pl.loop(0, 2 * blocks)
    def _(j):
        tile_copy(peer(far, j)[2]).wait_send()

    def drain(low, count):
        @pl.loop(1, 2 * blocks)
        def _(j):
            relay_copy(gy, peer(near, j)[2], count).wait_send()

        if not low:
            @pl.when(half == 0)
            def _():
                @pl.loop(0, 2 * blocks)
                def _(j):
                    relay_copy(gy, peer(far, j)[2], count).wait_send()

    at_ends(drain, True, False)


def solution(mesh):
    nx, ny = mesh.shape["gx"], mesh.shape["gy"]
    length = ny * TILE
    half = length // 2

    def body(velocity):
        out = pl.pallas_call(
            functools.partial(kernel, nx, ny),
            out_shape=jax.ShapeDtypeStruct((2 * ny, 2, ROWS, TILE), F32),
            in_specs=[pl.BlockSpec(memory_space=pl.ANY)] * 2,
            out_specs=pl.BlockSpec(memory_space=pltpu.VMEM),
            scratch_shapes=[
                pltpu.VMEM((4, ROWS, length), F32),
                pltpu.VMEM((ROWS, TILE), F32),
                pltpu.VMEM((len(NAMES), ROWS, TILE), F32),
                pltpu.VMEM((4, ROWS, length), F32),
                pltpu.VMEM((2, ROWS, length), F32),
                pltpu.VMEM((2, 4, ROWS, half), F32),
                pltpu.VMEM((2, ROWS, half), F32),
                pltpu.VMEM((2, ROWS, half), F32),
                pltpu.VMEM((2, ROWS, half), F32),
                pltpu.VMEM((2, 3, ROWS, half), F32),
                pltpu.VMEM((2, 3, ROWS, half), F32),
                pltpu.VMEM((2, ROWS, 2 * TILE), F32),
                pltpu.VMEM((2, ROWS, 2 * TILE), F32),
                pltpu.VMEM((4, 3, ROWS, half), F32),
                pltpu.VMEM((4, 3, ROWS, half), F32),
                pltpu.VMEM((4, ROWS, 2 * TILE), F32),
                pltpu.VMEM((4, ROWS, 2 * TILE), F32),
                pltpu.VMEM((4, ROWS, half), F32),
                pltpu.VMEM((ny, 5, ROWS, TILE), F32),
                pltpu.VMEM((ny, 5, ROWS, TILE), F32),
                pltpu.VMEM((ny, 3, ROWS, TILE), F32),
                pltpu.VMEM((ny, 3, ROWS, TILE), F32),
                pltpu.SemaphoreType.DMA((3,)),
                pltpu.SemaphoreType.DMA((2, 4 + ny // 2)),
                pltpu.SemaphoreType.DMA((4, 4 + ny // 2)),
                pltpu.SemaphoreType.DMA((ny,)),
                pltpu.SemaphoreType.DMA((ny,)),
                pltpu.SemaphoreType.DMA((ny,)),
                pltpu.SemaphoreType.DMA((ny,)),
                pltpu.SemaphoreType.REGULAR((ny // 4,)),
                pltpu.SemaphoreType.REGULAR((4,)),
                pltpu.SemaphoreType.REGULAR,
            ],
            compiler_params=pltpu.CompilerParams(collective_id=0, has_side_effects=True, vmem_limit_bytes=24576 * 1024),
        )(pltpu.with_memory_space_constraint(velocity, pltpu.HBM), pltpu.with_memory_space_constraint(jnp.asarray(COLUMNS), pltpu.HBM))
        return out.reshape(4 * ny, ROWS, TILE)

    return jax.shard_map(
        body, mesh=mesh, in_specs=(P("gy", "gx", None),), out_specs=P(None, "gx", "gy"), check_vma=False
    )
```
